32 devices in a mesh: ep: 16 (over z, y, core), dp: 2 (over x).
Axes of the slice: x: 2, y: 2, z: 4, core: 2. Of those that a mesh axis runs over, the one named last changes fastest.
Arguments:
- gradients: float32 [2, 2048, 7168], P('dp', 'ep'), may hold values from -18 to 18
- master_rows: float32 [16, 192, 7168], P('ep', 'dp'), may hold values from -0.24 to 0.24
- first_moment: float32 [16, 192, 7168], P('ep', 'dp'), may hold values from -2 to 2
- second_moment: float32 [16, 192, 7168], P('ep', 'dp'), may hold values from 0.1 to 1
- shard_rows: int32 [16, 2], replicated, may hold values from 1 to 96, as said below
- move_partner: int32 [16], replicated, may hold values from 0 to 15, as said below
Outputs:
- new_master: float32 [16, 192, 7168], P('ep', 'dp')
- new_first: float32 [16, 192, 7168], P('ep', 'dp')
- new_second: float32 [16, 192, 7168], P('ep', 'dp')
- placed_params: bfloat16 [2048, 7168], P('ep')
The draws below stay inside these ranges and needn't reach their ends.
Inputs may be any that keep to these rules, and one draw needn't show every extreme that they name: `shard_rows`: in each row the shards own consecutive runs of the 128 flat rows in order, each at least one row, summing to 128; the largest of each row is exactly 96. move_partner[i] is i or i with one binary digit flipped; that digit is the same for every i that moves; move_partner[move_partner[i]] == i.
All inputs are finite; a program needn't handle non-finite values.
Results may differ from the reference program's by a relative error of at most 0.014.
Values may be sent and summed in bfloat16 or wider, within the bound.
A program may use at most 128 MiB of HBM per device.

```python
import math
import jax
import jax.numpy as jnp
from jax import lax

D = 7168
FLAT = 128
CAP = 96
N_EP = 16
N_DP = 2


def draw_move_partner(key, part):
    indices = jnp.arange(N_EP, dtype=jnp.int32)
    bit_count = int(N_EP).bit_length() - 1
    key_bit, key_coin = jax.random.split(key)
    chosen = jax.random.randint(key_bit, (), 0, bit_count, dtype=jnp.int32)
    other_side = jnp.bitwise_xor(indices, jnp.left_shift(jnp.int32(1), chosen))
    lower = jnp.minimum(indices, other_side)
    coins = jax.random.randint(key_coin, (N_EP,), 0, 2, dtype=jnp.int32)
    partner = jnp.where(coins[lower] == 1, other_side, indices)
    return partner.astype(jnp.int32)


def shard_row_counts(row_key):
    key_place, key_spread = jax.random.split(row_key)
    indices = jnp.arange(N_DP, dtype=jnp.int32)
    largest = jax.random.randint(key_place, (), 0, N_DP, dtype=jnp.int32)
    counts = jnp.where(indices == largest, CAP, 1).astype(jnp.int32)
    room = jnp.where(indices == largest, 0, CAP - 1).astype(jnp.int32)
    extra = FLAT - CAP - (N_DP - 1)

    def spread_one(step, carry):
        current, left = carry
        scores = jax.random.randint(jax.random.fold_in(key_spread, step), (N_DP,), 0, 1024, dtype=jnp.int32) * N_DP + indices
        scores = jnp.where(left > 0, scores, -1)
        picked = jnp.argmax(scores).astype(jnp.int32)
        hit = (indices == picked).astype(jnp.int32)
        return (current + hit, left - hit)
    counts, room = lax.fori_loop(0, extra, spread_one, (counts, room))
    return counts.astype(jnp.int32)


def draw_shard_rows(key, part):
    row_keys = jax.random.split(jax.random.fold_in(key, 17), N_EP)
    return jax.vmap(shard_row_counts)(row_keys).astype(jnp.int32)


def level_of(key, dims, cuts, smallest, top_value):
    loudness, own = 1.0, jax.random.fold_in(key, 6)
    for dim, shards_of in cuts:
        steps = jnp.exp(jax.random.uniform(jax.random.fold_in(own, dim), (shards_of,), jnp.float32, smallest / len(cuts), top_value / len(cuts)))
        loudness = loudness * jnp.repeat(steps, dims[dim] // shards_of).reshape([-1 if axis == dim else 1 for axis in range(len(dims))])
    return loudness


def centred(own_key, extent, scale, limit, cuts=(), held_as=jnp.bfloat16):
    result = jax.random.normal(own_key, extent, jnp.float32) * scale
    if len(cuts) > 0:
        result = level_of(own_key, extent, cuts, -0.22, 0.18) * result
    return jnp.clip(result, min=-limit, max=limit).astype(held_as)


def setup_inputs(seed: int = 0) -> dict:
    key_of = jax.random.split(jax.random.key(seed), 7)
    gradients = centred(key_of[0], (N_DP, N_EP * FLAT, D), 3.0, 18.0, ((0, 2), (1, 16)), jnp.float32)
    master_rows = centred(key_of[1], (N_EP, N_DP * CAP, D), 0.04, 0.24, ((0, 16), (1, 2)), jnp.float32)
    first_moment = centred(key_of[2], (N_EP, N_DP * CAP, D), 0.3, 2.0, ((0, 16), (1, 2)), jnp.float32)
    second_moment = jnp.clip(jnp.exp(math.log(1.0) - 2.3025851 * jax.random.uniform(key_of[3], (N_EP, N_DP * CAP, D), jnp.float32) ** level_of(key_of[3], (N_EP, N_DP * CAP, D), ((0, 16), (1, 2)), -0.2, 0.2)), 0.1, 1.0)
    shard_rows = draw_shard_rows(jax.random.fold_in(key_of[6], 71), 0)
    move_partner = draw_move_partner(jax.random.fold_in(key_of[6], 71), 0)
    return {"gradients": gradients, "master_rows": master_rows, "first_moment": first_moment, "second_moment": second_moment, "shard_rows": shard_rows, "move_partner": move_partner}


beta_one = 0.9
beta_two = 0.95
learn_rate = 0.02
weight_decay = 0.1
epsilon = 1e-08
correct_one = 1.0 - 0.9 ** 10
correct_two = 1.0 - 0.95 ** 10

def adam_step(grad_rows, weights, first, second, live):
    first_new = beta_one * first + (1.0 - beta_one) * grad_rows
    second_new = beta_two * second + (1.0 - beta_two) * grad_rows * grad_rows
    ratio = first_new / correct_one / (jnp.sqrt(second_new / correct_two) + epsilon)
    updated = weights - learn_rate * (ratio + weight_decay * weights)
    return (jnp.where(live, updated, 0.0), jnp.where(live, first_new, 0.0), jnp.where(live, second_new, 0.0))

def one_group(grad_group, master_group, first_group, second_group, counts):
    starts = (jnp.cumsum(counts) - counts).astype(jnp.int32)
    slots = jnp.arange(N_DP * CAP, dtype=jnp.int32)
    owners = slots // CAP
    within = slots % CAP
    live = within < counts[owners]
    source = jnp.minimum(starts[owners] + within, FLAT - 1).astype(jnp.int32)
    grad_pad = jnp.where(live[:, None], grad_group[source, :], 0.0)
    return adam_step(grad_pad, master_group, first_group, second_group, live[:, None])

def place_group(master_group, counts):
    starts = (jnp.cumsum(counts) - counts).astype(jnp.int32)
    flat_rows = jnp.arange(FLAT, dtype=jnp.int32)
    owner_flat = lax.optimization_barrier(jnp.sum((flat_rows[:, None] >= starts[None, 1:]).astype(jnp.int32), axis=1)).astype(jnp.int32)
    position = (owner_flat * CAP + flat_rows - starts[owner_flat]).astype(jnp.int32)
    return master_group[position, :]

def reference(gradients, master_rows, first_moment, second_moment, shard_rows, move_partner):
    counts = shard_rows.astype(jnp.int32)
    grad_mean = (lax.optimization_barrier(jnp.sum(gradients, axis=0)) / N_DP).reshape(N_EP, FLAT, D)
    updated, first_new, second_new = jax.vmap(one_group)(grad_mean, master_rows, first_moment, second_moment, counts)
    new_master = updated[move_partner]
    new_first = first_new[move_partner]
    new_second = second_new[move_partner]
    moved_counts = counts[move_partner]
    placed = jax.vmap(place_group)(new_master, moved_counts).astype(jnp.bfloat16).reshape(N_EP * FLAT, D)
    return (new_master, new_first, new_second, placed)
```

```python
import functools

import jax
import jax.numpy as jnp
from jax import lax
from jax.experimental import pallas as pl
from jax.experimental.pallas import tpu as pltpu
from jax.sharding import PartitionSpec as P

beta_one = 0.9
beta_two = 0.95
learn_rate = 0.02
weight_decay = 0.1
epsilon = 1e-08
correct_one = 1.0 - 0.9**10
correct_two = 1.0 - 0.95**10


def swapped(array, axis, apart):
    return lax.ppermute(array, axis, [(i, i ^ 1 << apart) for i in range(lax.axis_size(axis))])


def adam_step(grad_rows, weights, first, second, live):
    first_new = beta_one * first + (1.0 - beta_one) * grad_rows
    second_new = beta_two * second + (1.0 - beta_two) * grad_rows * grad_rows
    ratio = first_new / correct_one / (jnp.sqrt(second_new / correct_two) + epsilon)
    updated = weights - learn_rate * (ratio + weight_decay * weights)
    return (
        jnp.where(live, updated, 0.0),
        jnp.where(live, first_new, 0.0),
        jnp.where(live, second_new, 0.0),
    )


def chosen_case(move_partner):
    count = move_partner.shape[0]
    flips = jnp.bitwise_xor(move_partner, jnp.arange(count, dtype=jnp.int32))
    digit = jnp.max(flips)
    return sum((digit >= 1 << bit).astype(jnp.int32) for bit in range(1, count.bit_length() - 1))


def move_new(values, partner, ep_index, move_partner):
    bits = lax.axis_size("ep").bit_length() - 1

    def exchange(bit_index):
        def run(values):
            arrived = swapped(values.astype(jnp.bfloat16), "ep", bit_index)
            return jnp.where(partner == ep_index, values, arrived.astype(values.dtype))
        return run

    return lax.switch(
        chosen_case(move_partner), [exchange(bit_index) for bit_index in range(bits)], values
    )


def pick(rows, columns, start, count, slots_first):
    shape = (rows, columns)
    slot = lax.broadcasted_iota(jnp.int32, shape, 0 if slots_first else 1)
    flat = lax.broadcasted_iota(jnp.int32, shape, 1 if slots_first else 0)
    hit = jnp.logical_and(flat == slot + start, slot < count)
    return jnp.where(hit, 1.0, 0.0).astype(jnp.bfloat16)


def fused_kernel(
    bit, counts_ref, partner_ref, grad_hbm, master_hbm, first_hbm, second_hbm,
    new_hbm, placed_hbm,
    grad, state, grad_out, grad_in, new_out, new_in, params_in, placed,
    load_sem, grad_send, grad_recv, new_send, new_recv, params_send, params_recv,
    store_sem, placed_sem,
):
    parts, flat_count, width = grad.shape
    capacity = state.shape[2]
    ep_index, dp_index = lax.axis_index("ep"), lax.axis_index("dp")
    step = 1 << bit
    mate = ep_index + step * (1 - 2 * ((ep_index // step) % 2))
    to_peer, to_mate = {"dp": 1 - dp_index}, {"ep": mate}
    mesh_ids = pl.DeviceIdType.MESH

    def columns(part):
        return pl.ds(pl.multiple_of(part * width, width), width)

    def load(part, index):
        source = (grad_hbm, master_hbm, first_hbm, second_hbm)[index]
        target = grad.at[part] if index == 0 else state.at[part, index - 1]
        return pltpu.make_async_copy(
            source.at[:, columns(part)], target, load_sem.at[index, part])

    def send_grad(part):
        return pltpu.make_async_remote_copy(
            grad_out.at[part], grad_in.at[part], grad_send.at[part], grad_recv.at[part],
            device_id=to_peer, device_id_type=mesh_ids)

    def send_new(part):
        return pltpu.make_async_remote_copy(
            new_out.at[part], new_in.at[part], new_send.at[part], new_recv.at[part],
            device_id=to_mate, device_id_type=mesh_ids)

    def send_params(part):
        return pltpu.make_async_remote_copy(
            new_in.at[part, 0], params_in.at[part], params_send.at[part], params_recv.at[part],
            device_id=to_peer, device_id_type=mesh_ids)

    def store_new(part):
        return pltpu.make_async_copy(
            new_in.at[part], new_hbm.at[:, :, columns(part)], store_sem.at[part])

    def store_placed(part):
        return pltpu.make_async_copy(
            placed.at[part], placed_hbm.at[:, columns(part)], placed_sem.at[part])

    def each(step_of):
        def run(part, carry):
            step_of(part)
            return carry
        lax.fori_loop(0, parts, run, 0)

    @each
    def _(part):
        for index in range(4):
            load(part, index).start()

    barrier = pltpu.get_barrier_semaphore()
    pl.semaphore_signal(barrier, inc=1, device_id=to_peer, device_id_type=mesh_ids)
    pl.semaphore_signal(barrier, inc=1, device_id=to_mate, device_id_type=mesh_ids)
    pl.semaphore_wait(barrier, 2)

    first_count = counts_ref[ep_index, 0]
    own_start = dp_index * first_count
    peer_start = first_count - own_start
    own_count = counts_ref[ep_index, dp_index]
    peer_count = counts_ref[ep_index, 1 - dp_index]
    pick_own = pick(capacity, flat_count, own_start, own_count, True)
    pick_peer = pick(capacity, flat_count, peer_start, peer_count, True)
    live = lax.broadcasted_iota(jnp.int32, (capacity, width), 0) < own_count

    @each
    def _(part):
        load(part, 0).wait()
        grad_out[part] = jnp.dot(
            pick_peer, grad[part].astype(jnp.bfloat16), preferred_element_type=jnp.float32
        ).astype(jnp.bfloat16)
        send_grad(part).start()

    @each
    def _(part):
        own = jnp.dot(
            pick_own, grad[part].astype(jnp.bfloat16), preferred_element_type=jnp.float32)
        for index in range(1, 4):
            load(part, index).wait()
        send_grad(part).wait_recv()
        grad_mean = (own + grad_in[part].astype(jnp.float32)) / 2
        results = adam_step(grad_mean, state[part, 0], state[part, 1], state[part, 2], live)
        for index, result in enumerate(results):
            new_out[part, index] = result.astype(jnp.bfloat16)
        send_new(part).start()

    source = partner_ref[ep_index]
    moves = jnp.broadcast_to(source, (capacity, width)) != ep_index
    placed_first = counts_ref[source, 0]
    own_place = pick(
        flat_count, capacity, dp_index * placed_first, counts_ref[source, dp_index], False)
    peer_place = pick(
        flat_count, capacity, (1 - dp_index) * placed_first, counts_ref[source, 1 - dp_index],
        False)

    def arrive(part):
        send_new(part).wait_recv()
        for index in range(3):
            new_in[part, index] = jnp.where(
                moves,
                new_in[part, index].astype(jnp.float32),
                new_out[part, index].astype(jnp.float32),
            ).astype(jnp.bfloat16)
        send_params(part).start()
        store_new(part).start()

    def place(part):
        send_params(part).wait_recv()
        placed[part] = (
            jnp.dot(own_place, new_in[part, 0], preferred_element_type=jnp.float32)
            + jnp.dot(peer_place, params_in[part], preferred_element_type=jnp.float32)
        ).astype(jnp.bfloat16)
        store_placed(part).start()

    arrive(0)

    def pair(part, carry):
        arrive(part)
        place(part - 1)
        return carry

    lax.fori_loop(1, parts, pair, 0)
    place(parts - 1)

    @each
    def _(part):
        send_grad(part).wait_send()
        send_new(part).wait_send()
        send_params(part).wait_send()
        store_new(part).wait()
        store_placed(part).wait()


def fused(bit, counts, partner, gradients, master, first, second):
    flat_count, model = gradients.shape
    capacity = master.shape[0]
    width = 512
    parts = model // width
    low, high = jnp.bfloat16, jnp.float32
    sems = pltpu.SemaphoreType.DMA((parts,))
    smem = pl.BlockSpec(memory_space=pltpu.SMEM)
    anywhere = pl.BlockSpec(memory_space=pl.ANY)
    return pl.pallas_call(
        functools.partial(fused_kernel, bit),
        out_shape=(
            jax.ShapeDtypeStruct((3, capacity, model), low),
            jax.ShapeDtypeStruct((flat_count, model), low),
        ),
        in_specs=[smem, smem] + [anywhere] * 4,
        out_specs=(anywhere, anywhere),
        scratch_shapes=[
            pltpu.VMEM((parts, flat_count, width), high),
            pltpu.VMEM((parts, 3, capacity, width), high),
            pltpu.VMEM((parts, capacity, width), low),
            pltpu.VMEM((parts, capacity, width), low),
            pltpu.VMEM((parts, 3, capacity, width), low),
            pltpu.VMEM((parts, 3, capacity, width), low),
            pltpu.VMEM((parts, capacity, width), low),
            pltpu.VMEM((parts, flat_count, width), low),
            pltpu.SemaphoreType.DMA((4, parts)),
        ] + [sems] * 8,
        compiler_params=pltpu.CompilerParams(
            collective_id=bit, has_side_effects=True, vmem_limit_bytes=48 * 1024 * 1024),
        name=f"fused_bit_{bit}",
    )(counts, partner, gradients, master, first, second)


def body_pairs(gradients, master_rows, first_moment, second_moment, shard_rows, move_partner):
    bits = lax.axis_size("ep").bit_length() - 1
    moved, placed = lax.switch(
        chosen_case(move_partner),
        [functools.partial(fused, bit) for bit in range(bits)],
        shard_rows, move_partner, gradients[0], master_rows[0], first_moment[0], second_moment[0],
    )
    wide = moved.astype(jnp.float32)
    return (wide[0][None], wide[1][None], wide[2][None], placed)


def body(gradients, master_rows, first_moment, second_moment, shard_rows, move_partner):
    groups = lax.axis_size("dp")
    capacity = master_rows.shape[1]
    flat_count = gradients.shape[1]
    dp_index = lax.axis_index("dp")
    ep_index = lax.axis_index("ep")
    partner = move_partner[ep_index]
    counts = shard_rows[ep_index]
    moved_counts = shard_rows[partner]
    starts = jnp.cumsum(counts) - counts
    moved_starts = jnp.cumsum(moved_counts) - moved_counts
    own_slots = jnp.arange(capacity, dtype=jnp.int32)
    live = (own_slots < counts[dp_index])[:, None]
    state = jnp.stack([master_rows[0], first_moment[0], second_moment[0]])
    slots = jnp.arange(groups * capacity, dtype=jnp.int32)
    owners = slots // capacity
    within = slots % capacity
    live_all = (within < counts[owners])[:, None]
    source = jnp.minimum(starts[owners] + within, flat_count - 1)
    packed = jnp.where(live_all, jnp.take(gradients[0], source, axis=0), 0.0)
    summed = lax.psum_scatter(
        packed.astype(jnp.bfloat16), "dp", scatter_dimension=0, tiled=True
    ).astype(jnp.float32)
    grad_own = summed / groups
    updated, first_new, second_new = adam_step(grad_own, state[0], state[1], state[2], live)
    moved = move_new(jnp.stack([updated, first_new, second_new]), partner, ep_index, move_partner)
    updated, first_new, second_new = (moved[0], moved[1], moved[2])
    whole = lax.all_gather(updated.astype(jnp.bfloat16), "dp", axis=0, tiled=True)
    flat_rows = jnp.arange(flat_count, dtype=jnp.int32)
    owner_flat = jnp.sum((flat_rows[:, None] >= moved_starts[None, 1:]).astype(jnp.int32), axis=1)
    position = owner_flat * capacity + flat_rows - moved_starts[owner_flat]
    placed = jnp.take(whole, position, axis=0)
    return (updated[None], first_new[None], second_new[None], placed)


def solution(mesh):
    placed = (
        P("dp", "ep", None),
        P("ep", "dp", None),
        P("ep", "dp", None),
        P("ep", "dp", None),
        P(),
        P(),
    )
    return jax.shard_map(
        body_pairs if mesh.shape["dp"] == 2 else body,
        mesh=mesh,
        in_specs=placed,
        out_specs=(P("ep", "dp", None), P("ep", "dp", None), P("ep", "dp", None), P("ep", None)),
        check_vma=False,
    )
```

```python
import functools

import jax
import jax.numpy as jnp
from jax import lax
from jax.experimental import pallas as pl
from jax.experimental.pallas import tpu as pltpu
from jax.sharding import PartitionSpec as P

beta_one = 0.9
beta_two = 0.95
learn_rate = 0.02
weight_decay = 0.1
epsilon = 1e-08
correct_one = 1.0 - 0.9**10
correct_two = 1.0 - 0.95**10


def swapped(array, axis, apart):
    return lax.ppermute(array, axis, [(i, i ^ 1 << apart) for i in range(lax.axis_size(axis))])


def adam_step(grad_rows, weights, first, second):
    first_new = beta_one * first + (1.0 - beta_one) * grad_rows
    second_new = beta_two * second + (1.0 - beta_two) * grad_rows * grad_rows
    ratio = first_new / correct_one / (jnp.sqrt(second_new / correct_two) + epsilon)
    updated = weights - learn_rate * (ratio + weight_decay * weights)
    return updated, first_new, second_new


def chosen_case(move_partner):
    count = move_partner.shape[0]
    flips = jnp.bitwise_xor(move_partner, jnp.arange(count, dtype=jnp.int32))
    digit = jnp.max(flips)
    return sum((digit >= 1 << bit).astype(jnp.int32) for bit in range(1, count.bit_length() - 1))


def move_new(values, partner, ep_index, move_partner):
    bits = lax.axis_size("ep").bit_length() - 1

    def exchange(bit_index):
        def run(values):
            arrived = swapped(values.astype(jnp.bfloat16), "ep", bit_index)
            return jnp.where(partner == ep_index, values, arrived.astype(values.dtype))
        return run

    return lax.switch(
        chosen_case(move_partner), [exchange(bit_index) for bit_index in range(bits)], values
    )


def fused_kernel(
    bit, shifted, lag, counts_ref, partner_ref, grad_hbm, master_hbm, first_hbm, second_hbm,
    new_hbm, placed_hbm,
    grad, state, edge_out, edge_in, mid_out, mid_in, own_out, own_in, slot_out, slot_in,
    back_out, back_in, new, placed,
    load_sem, edge_send, edge_recv, mid_send, mid_recv, own_send, own_recv,
    slot_send, slot_recv, back_send, back_recv, new_sem, placed_sem,
):
    parts, flat_count, width = grad.shape
    capacity = state.shape[2]
    edge = flat_count - capacity
    middle = flat_count - 2 * edge
    kept = middle - shifted
    slot_rows = slot_out.shape[1] // 3
    shift_rows = 3 * shifted if shifted else middle
    low, high = jnp.bfloat16, jnp.float32
    ep_index, dp_index = lax.axis_index("ep"), lax.axis_index("dp")
    step = 1 << bit
    mate = ep_index + step * (1 - 2 * ((ep_index // step) % 2))
    to_peer, to_mate = {"dp": 1 - dp_index}, {"ep": mate}
    mesh_ids = pl.DeviceIdType.MESH

    def columns(part):
        return pl.ds(pl.multiple_of(part * width, width), width)

    def load(part, index):
        source = (grad_hbm, master_hbm, first_hbm, second_hbm)[index]
        target = grad.at[part] if index == 0 else state.at[part, index - 1]
        return pltpu.make_async_copy(
            source.at[:, columns(part)], target, load_sem.at[index, part])

    def remote(out, into, sent, received, target):
        def at(part):
            return pltpu.make_async_remote_copy(
                out.at[part], into.at[part], sent.at[part], received.at[part],
                device_id=target, device_id_type=mesh_ids)
        return at

    send_edge = remote(edge_out, edge_in, edge_send, edge_recv, to_peer)
    send_mid = remote(mid_out, mid_in, mid_send, mid_recv, to_peer)
    send_own = remote(own_out, own_in, own_send, own_recv, to_mate)
    send_slot = remote(slot_out, slot_in, slot_send, slot_recv, to_mate)
    send_back = remote(back_out, back_in, back_send, back_recv, to_peer)

    def store_new(part):
        return pltpu.make_async_copy(new.at[part], new_hbm.at[:, :, columns(part)], new_sem.at[part])

    def store_placed(part):
        return pltpu.make_async_copy(
            placed.at[part], placed_hbm.at[:, columns(part)], placed_sem.at[part])

    def each(count, step_of):
        def run(part, carry):
            step_of(part)
            return carry
        lax.fori_loop(0, count, run, 0)

    def start_loads(part):
        for index in range(4):
            load(part, index).start()

    each(parts, start_loads)

    barrier = pltpu.get_barrier_semaphore()
    pl.semaphore_signal(barrier, inc=1, device_id=to_peer, device_id_type=mesh_ids)
    pl.semaphore_signal(barrier, inc=1, device_id=to_mate, device_id_type=mesh_ids)
    pl.semaphore_wait(barrier, 2)

    source = partner_ref[ep_index]
    owns_value = counts_ref[ep_index, dp_index]
    moves_value = source
    owns_moved_value = counts_ref[source, dp_index]

    def full(value, rows):
        return jnp.broadcast_to(value, (rows, width))

    def owns(rows):
        return full(owns_value, rows) == capacity

    def owns_moved(rows):
        return full(owns_moved_value, rows) == capacity

    def moves(rows):
        return full(moves_value, rows) != ep_index

    def is_last(rows):
        return full(dp_index, rows) == 1

    def select(mask, one, other):
        return jnp.where(mask, one.astype(high), other.astype(high))

    own_edge = pl.ds(pl.multiple_of((flat_count - edge) * dp_index, edge), edge)
    peer_edge = pl.ds(pl.multiple_of((flat_count - edge) * (1 - dp_index), edge), edge)
    own_middle = pl.ds(pl.multiple_of(edge * (1 - dp_index), edge), middle)

    def update(part):
        send_edge(part).wait_recv()
        for index in range(1, 4):
            load(part, index).wait()
        edge_mean = (grad[part, own_edge] + edge_in[part].astype(high)) / 2
        late = jnp.logical_and(owns(edge), is_last(edge))
        edge_state = [
            jnp.where(late, state[part, index, capacity - edge:], state[part, index, :edge])
            for index in range(3)
        ]
        for index, result in enumerate(adam_step(edge_mean, *edge_state)):
            own_out[part, index * edge:(index + 1) * edge] = result.astype(low)
        send_own(part).start()
        middle_mean = (
            grad[part, edge:edge + middle] + mid_in[part, :middle].astype(high)) / 2
        middle_state = [state[part, index, own_middle] for index in range(3)]
        for index, result in enumerate(adam_step(middle_mean, *middle_state)):
            result = result.astype(low)
            slot_out[part, index * slot_rows:index * slot_rows + kept] = result[:kept]
            if shifted:
                mid_out[part + lag, index * shifted:(index + 1) * shifted] = result[kept:]
            elif index == 0:
                mid_out[part + lag, :middle] = result

    def front(turn):
        @pl.when(turn < parts)
        def _():
            load(turn, 0).wait()
            edge_out[turn] = grad[turn, peer_edge].astype(low)
            send_edge(turn).start()

        @pl.when(turn >= lag)
        def _():
            send_mid(turn - lag).wait_recv()

        @pl.when(jnp.logical_and(turn >= lag, turn < parts + lag))
        def _():
            update(turn - lag)

        @pl.when(turn < lag)
        def _():
            mid_out[turn, :middle] = grad[turn, edge:edge + middle].astype(low)

        @pl.when(jnp.logical_and(turn >= lag, turn < parts))
        def _():
            mid_out[turn, :middle] = select(
                owns(middle), mid_out[turn, :middle], grad[turn, edge:edge + middle]).astype(low)

        @pl.when(turn < parts + lag)
        def _():
            send_mid(turn).start()

        @pl.when(turn >= 2 * lag)
        def _():
            part = turn - 2 * lag
            pieces = [(index * slot_rows, index * shifted, shifted) for index in range(3)]
            for at, come, rows in pieces if shifted else [(0, 0, middle)]:
                slot_out[part, at:at + rows] = select(
                    owns(rows), slot_out[part, at:at + rows],
                    mid_in[turn - lag, come:come + rows]).astype(low)
            send_slot(part).start()

    each(parts + 2 * lag, front)

    def arrive(part):
        send_own(part).wait_recv()
        own_in[part] = select(moves(3 * edge), own_in[part], own_out[part]).astype(low)
        back_out[part, :edge] = own_in[part, :edge]
        send_slot(part).wait_recv()
        slot_in[part] = select(
            moves(3 * slot_rows), slot_in[part], slot_out[part]).astype(low)
        if shifted:
            for index in range(3):
                at = index * shifted
                back_out[part, edge + at:edge + at + shifted] = select(
                    owns_moved(shifted), slot_in[part, at:at + shifted],
                    slot_in[part, index * slot_rows:index * slot_rows + shifted]).astype(low)
        send_back(part).start()

    def place(part):
        send_back(part).wait_recv()
        keeps, last = owns_moved(edge), is_last(edge)
        zero = jnp.zeros((edge, width), high)
        for index in range(3):
            held = slot_in[part, index * slot_rows:index * slot_rows + kept].astype(high)
            if shifted:
                rest = back_in[part, edge + index * shifted:edge + (index + 1) * shifted]
                moved = jnp.concatenate([held, rest.astype(high)], axis=0)
            else:
                moved = held
            ends = own_in[part, index * edge:(index + 1) * edge].astype(high)
            low_half, high_half = moved[:edge], moved[edge:]
            new[part, index, :edge] = jnp.where(
                jnp.logical_and(keeps, last), low_half, ends).astype(low)
            new[part, index, edge:2 * edge] = jnp.where(
                keeps, jnp.where(last, high_half, low_half), zero).astype(low)
            new[part, index, 2 * edge:] = jnp.where(
                keeps, jnp.where(last, ends, high_half), zero).astype(low)
            if index == 0:
                if shifted:
                    other = jnp.concatenate([
                        back_in[part, edge:edge + kept].astype(high),
                        slot_in[part, :shifted].astype(high)], axis=0)
                    moved = jnp.where(owns_moved(middle), moved, other)
                placed[part, edge:edge + middle] = moved.astype(low)
                peer_ends = back_in[part, :edge].astype(high)
                placed[part, :edge] = jnp.where(last, peer_ends, ends).astype(low)
                placed[part, edge + middle:] = jnp.where(last, ends, peer_ends).astype(low)
        store_new(part).start()
        store_placed(part).start()

    def back(turn):
        @pl.when(turn < parts)
        def _():
            arrive(turn)

        @pl.when(turn > 0)
        def _():
            place(turn - 1)

    each(parts + 1, back)

    def finish(part):
        send_edge(part).wait_send()
        send_own(part).wait_send()
        send_slot(part).wait_send()
        send_back(part).wait_send()
        store_new(part).wait()
        store_placed(part).wait()

    each(parts, finish)
    each(parts + lag, lambda part: send_mid(part).wait_send())


def fused(bit, shifted, counts, partner, gradients, master, first, second):
    flat_count, model = gradients.shape
    capacity = master.shape[0]
    edge = flat_count - capacity
    middle = flat_count - 2 * edge
    kept = middle - shifted
    width, lag = 512, 2
    parts = model // width
    mid_rows = max(middle, 3 * shifted)
    slot_rows = 3 * max(kept, shifted)
    back_rows = edge + (max(kept, 3 * shifted) if shifted else 0)
    low, high = jnp.bfloat16, jnp.float32
    sems, more_sems = (pltpu.SemaphoreType.DMA((count,)) for count in (parts, parts + lag))
    smem = pl.BlockSpec(memory_space=pltpu.SMEM)
    anywhere = pl.BlockSpec(memory_space=pl.ANY)

    def pair(count, rows):
        return [pltpu.VMEM((count, rows, width), low)] * 2

    return pl.pallas_call(
        functools.partial(fused_kernel, bit, shifted, lag),
        out_shape=(
            jax.ShapeDtypeStruct((3, capacity, model), low),
            jax.ShapeDtypeStruct((flat_count, model), low),
        ),
        in_specs=[smem, smem] + [anywhere] * 4,
        out_specs=(anywhere, anywhere),
        scratch_shapes=[
            pltpu.VMEM((parts, flat_count, width), high),
            pltpu.VMEM((parts, 3, capacity, width), high),
        ] + pair(parts, edge) + pair(parts + lag, mid_rows) + pair(parts, 3 * edge)
        + pair(parts, slot_rows) + pair(parts, back_rows) + [
            pltpu.VMEM((parts, 3, capacity, width), low),
            pltpu.VMEM((parts, flat_count, width), low),
            pltpu.SemaphoreType.DMA((4, parts)),
        ] + [sems] * 2 + [more_sems] * 2 + [sems] * 8,
        compiler_params=pltpu.CompilerParams(
            collective_id=bit, has_side_effects=True, vmem_limit_bytes=56 * 1024 * 1024),
        name=f"fused_bit_{bit}",
    )(counts, partner, gradients, master, first, second)


def body_pairs(gradients, master_rows, first_moment, second_moment, shard_rows, move_partner):
    bits = lax.axis_size("ep").bit_length() - 1
    moved, placed = lax.switch(
        chosen_case(move_partner),
        [functools.partial(fused, bit, (0, 16, 16, 32)[bit]) for bit in range(bits)],
        shard_rows, move_partner, gradients[0], master_rows[0], first_moment[0], second_moment[0],
    )
    wide = moved.astype(jnp.float32)
    return (wide[0][None], wide[1][None], wide[2][None], placed)


def body(gradients, master_rows, first_moment, second_moment, shard_rows, move_partner):
    groups = lax.axis_size("dp")
    capacity = master_rows.shape[1]
    flat_count = gradients.shape[1]
    dp_index = lax.axis_index("dp")
    ep_index = lax.axis_index("ep")
    partner = move_partner[ep_index]
    counts = shard_rows[ep_index]
    moved_counts = shard_rows[partner]
    starts = jnp.cumsum(counts) - counts
    moved_starts = jnp.cumsum(moved_counts) - moved_counts
    own_slots = jnp.arange(capacity, dtype=jnp.int32)
    live = (own_slots < counts[dp_index])[:, None]
    state = jnp.stack([master_rows[0], first_moment[0], second_moment[0]])
    slots = jnp.arange(groups * capacity, dtype=jnp.int32)
    owners = slots // capacity
    within = slots % capacity
    live_all = (within < counts[owners])[:, None]
    source = jnp.minimum(starts[owners] + within, flat_count - 1)
    packed = jnp.where(live_all, jnp.take(gradients[0], source, axis=0), 0.0)
    summed = lax.psum_scatter(
        packed.astype(jnp.bfloat16), "dp", scatter_dimension=0, tiled=True
    ).astype(jnp.float32)
    grad_own = summed / groups
    stepped = jnp.where(live, jnp.stack(adam_step(grad_own, state[0], state[1], state[2])), 0.0)
    moved = move_new(stepped, partner, ep_index, move_partner)
    updated, first_new, second_new = (moved[0], moved[1], moved[2])
    whole = lax.all_gather(updated.astype(jnp.bfloat16), "dp", axis=0, tiled=True)
    flat_rows = jnp.arange(flat_count, dtype=jnp.int32)
    owner_flat = jnp.sum((flat_rows[:, None] >= moved_starts[None, 1:]).astype(jnp.int32), axis=1)
    position = owner_flat * capacity + flat_rows - moved_starts[owner_flat]
    placed = jnp.take(whole, position, axis=0)
    return (updated[None], first_new[None], second_new[None], placed)


def solution(mesh):
    placed = (
        P("dp", "ep", None),
        P("ep", "dp", None),
        P("ep", "dp", None),
        P("ep", "dp", None),
        P(),
        P(),
    )
    return jax.shard_map(
        body_pairs if mesh.shape["dp"] == 2 else body,
        mesh=mesh,
        in_specs=placed,
        out_specs=(P("ep", "dp", None), P("ep", "dp", None), P("ep", "dp", None), P("ep", None)),
        check_vma=False,
    )
```

```python
import functools

import jax
import jax.numpy as jnp
from jax import lax
from jax.experimental import pallas as pl
from jax.experimental.pallas import tpu as pltpu
from jax.sharding import PartitionSpec as P

beta_one = 0.9
beta_two = 0.95
learn_rate = 0.02
weight_decay = 0.1
epsilon = 1e-08
shifts_of_bit = ((0,), (16, 32), (16, 32), (32,))
correct_one = 1.0 - 0.9**10
correct_two = 1.0 - 0.95**10


def swapped(array, axis, apart):
    return lax.ppermute(array, axis, [(i, i ^ 1 << apart) for i in range(lax.axis_size(axis))])


def adam_step(grad_rows, weights, first, second):
    first_new = beta_one * first + (1.0 - beta_one) * grad_rows
    second_new = beta_two * second + (1.0 - beta_two) * grad_rows * grad_rows
    ratio = first_new / correct_one / (jnp.sqrt(second_new / correct_two) + epsilon)
    updated = weights - learn_rate * (ratio + weight_decay * weights)
    return updated, first_new, second_new


def chosen_case(move_partner):
    count = move_partner.shape[0]
    flips = jnp.bitwise_xor(move_partner, jnp.arange(count, dtype=jnp.int32))
    digit = jnp.max(flips)
    return sum((digit >= 1 << bit).astype(jnp.int32) for bit in range(1, count.bit_length() - 1))


def move_new(values, partner, ep_index, move_partner):
    bits = lax.axis_size("ep").bit_length() - 1

    def exchange(bit_index):
        def run(values):
            arrived = swapped(values.astype(jnp.bfloat16), "ep", bit_index)
            return jnp.where(partner == ep_index, values, arrived.astype(values.dtype))
        return run

    return lax.switch(
        chosen_case(move_partner), [exchange(bit_index) for bit_index in range(bits)], values
    )


def fused_kernel(
    bit, shifts, lag, counts_ref, partner_ref, grad_hbm, master_hbm, first_hbm, second_hbm,
    new_hbm, placed_hbm,
    grad, state, edge_out, edge_in, mid_out, mid_in, own_out, own_in, slot_out, slot_in,
    back_out, back_in, new, placed,
    load_sem, edge_send, edge_recv, mid_send, mid_recv, own_send, own_recv,
    slot_send, slot_recv, back_send, back_recv, new_sem, placed_sem,
):
    parts, flat_count, width = grad.shape
    capacity = state.shape[2]
    edge = flat_count - capacity
    middle = flat_count - 2 * edge
    low, high = jnp.bfloat16, jnp.float32
    ep_index, dp_index = lax.axis_index("ep"), lax.axis_index("dp")
    step = 1 << bit
    mate = ep_index + step * (1 - 2 * ((ep_index // step) % 2))
    to_peer, to_mate = {"dp": 1 - dp_index}, {"ep": mate}
    mesh_ids = pl.DeviceIdType.MESH

    def columns(part):
        return pl.ds(pl.multiple_of(part * width, width), width)

    def load(part, index):
        source = (grad_hbm, master_hbm, first_hbm, second_hbm)[index]
        target = grad.at[part] if index == 0 else state.at[part, index - 1]
        return pltpu.make_async_copy(
            source.at[:, columns(part)], target, load_sem.at[index, part])

    def remote(part, rows, out, into, sent, received, target):
        return pltpu.make_async_remote_copy(
            out.at[part, :rows], into.at[part, :rows], sent.at[part], received.at[part],
            device_id=target, device_id_type=mesh_ids)

    def send_edge(part):
        return remote(part, edge, edge_out, edge_in, edge_send, edge_recv, to_peer)

    def send_mid(part, shifted):
        rows = max(middle, 3 * shifted)
        return remote(part, rows, mid_out, mid_in, mid_send, mid_recv, to_peer)

    def send_own(part):
        return remote(part, 3 * edge, own_out, own_in, own_send, own_recv, to_mate)

    def send_slot(part, shifted):
        rows = 3 * max(middle - shifted, shifted)
        return remote(part, rows, slot_out, slot_in, slot_send, slot_recv, to_mate)

    def send_back(part, shifted):
        rows = edge + (max(middle - shifted, 3 * shifted) if shifted else 0)
        return remote(part, rows, back_out, back_in, back_send, back_recv, to_peer)

    def store_new(part):
        return pltpu.make_async_copy(new.at[part], new_hbm.at[:, :, columns(part)], new_sem.at[part])

    def store_placed(part):
        return pltpu.make_async_copy(
            placed.at[part], placed_hbm.at[:, columns(part)], placed_sem.at[part])

    def each(count, step_of):
        def run(group, carry):
            for index, shifted in enumerate(shifts):
                step_of(group * len(shifts) + index, shifted)
            return carry
        lax.fori_loop(0, -(-count // len(shifts)), run, 0)

    def start_loads(part, _):
        for index in range(4):
            load(part, index).start()

    each(parts, start_loads)

    barrier = pltpu.get_barrier_semaphore()
    pl.semaphore_signal(barrier, inc=1, device_id=to_peer, device_id_type=mesh_ids)
    pl.semaphore_signal(barrier, inc=1, device_id=to_mate, device_id_type=mesh_ids)
    pl.semaphore_wait(barrier, 2)

    source = partner_ref[ep_index]
    owns_value = counts_ref[ep_index, dp_index]
    moves_value = source
    owns_moved_value = counts_ref[source, dp_index]

    def full(value, rows):
        return jnp.broadcast_to(value, (rows, width))

    def owns(rows):
        return full(owns_value, rows) == capacity

    def owns_moved(rows):
        return full(owns_moved_value, rows) == capacity

    def moves(rows):
        return full(moves_value, rows) != ep_index

    def is_last(rows):
        return full(dp_index, rows) == 1

    def select(mask, one, other):
        return jnp.where(mask, one.astype(high), other.astype(high))

    own_edge = pl.ds(pl.multiple_of((flat_count - edge) * dp_index, edge), edge)
    peer_edge = pl.ds(pl.multiple_of((flat_count - edge) * (1 - dp_index), edge), edge)
    own_middle = pl.ds(pl.multiple_of(edge * (1 - dp_index), edge), middle)

    def update_edge(part):
        send_edge(part).wait_recv()
        for index in range(1, 4):
            load(part, index).wait()
        edge_mean = (grad[part, own_edge] + edge_in[part].astype(high)) / 2
        late = jnp.logical_and(owns(edge), is_last(edge))
        edge_state = [
            jnp.where(late, state[part, index, capacity - edge:], state[part, index, :edge])
            for index in range(3)
        ]
        for index, result in enumerate(adam_step(edge_mean, *edge_state)):
            own_out[part, index * edge:(index + 1) * edge] = result.astype(low)
        send_own(part).start()

    def update_middle(part, shifted):
        kept = middle - shifted
        slot_rows = max(kept, shifted)
        middle_mean = (
            grad[part, edge:edge + middle] + mid_in[part, :middle].astype(high)) / 2
        middle_state = [state[part, index, own_middle] for index in range(3)]
        for index, result in enumerate(adam_step(middle_mean, *middle_state)):
            result = result.astype(low)
            slot_out[part, index * slot_rows:index * slot_rows + kept] = result[:kept]
            if shifted:
                mid_out[part + lag, index * shifted:(index + 1) * shifted] = result[kept:]
            elif index == 0:
                mid_out[part + lag, :middle] = result

    def front(turn, shifted):
        @pl.when(turn < parts)
        def _():
            load(turn, 0).wait()
            edge_out[turn] = grad[turn, peer_edge].astype(low)
            send_edge(turn).start()

        @pl.when(turn >= lag)
        def _():
            send_mid(turn - lag, shifted).wait_recv()

        @pl.when(jnp.logical_and(turn >= lag, turn < parts + lag))
        def _():
            update_middle(turn - lag, shifted)

        @pl.when(turn < lag)
        def _():
            mid_out[turn, :middle] = grad[turn, edge:edge + middle].astype(low)

        @pl.when(jnp.logical_and(turn >= lag, turn < parts))
        def _():
            mid_out[turn, :middle] = select(
                owns(middle), mid_out[turn, :middle], grad[turn, edge:edge + middle]).astype(low)

        @pl.when(turn < parts + lag)
        def _():
            send_mid(turn, shifted).start()

        @pl.when(jnp.logical_and(turn >= 1, turn < parts + 1))
        def _():
            update_edge(turn - 1)

        @pl.when(turn >= 2 * lag)
        def _():
            part = turn - 2 * lag
            slot_rows = max(middle - shifted, shifted)
            pieces = [(index * slot_rows, index * shifted, shifted) for index in range(3)]
            for at, come, rows in pieces if shifted else [(0, 0, middle)]:
                slot_out[part, at:at + rows] = select(
                    owns(rows), slot_out[part, at:at + rows],
                    mid_in[turn - lag, come:come + rows]).astype(low)
            send_slot(part, shifted).start()

    each(parts + 2 * lag, front)

    def arrive(part, shifted):
        slot_rows = max(middle - shifted, shifted)
        send_own(part).wait_recv()
        own_in[part] = select(moves(3 * edge), own_in[part], own_out[part]).astype(low)
        back_out[part, :edge] = own_in[part, :edge]
        send_slot(part, shifted).wait_recv()
        rows = 3 * slot_rows
        slot_in[part, :rows] = select(
            moves(rows), slot_in[part, :rows], slot_out[part, :rows]).astype(low)
        if shifted:
            for index in range(3):
                at = index * shifted
                back_out[part, edge + at:edge + at + shifted] = select(
                    owns_moved(shifted), slot_in[part, at:at + shifted],
                    slot_in[part, index * slot_rows:index * slot_rows + shifted]).astype(low)
        send_back(part, shifted).start()

    def place(part, shifted):
        kept = middle - shifted
        slot_rows = max(kept, shifted)
        send_back(part, shifted).wait_recv()
        keeps, last = owns_moved(edge), is_last(edge)
        zero = jnp.zeros((edge, width), high)
        for index in range(3):
            held = slot_in[part, index * slot_rows:index * slot_rows + kept].astype(high)
            if shifted:
                rest = back_in[part, edge + index * shifted:edge + (index + 1) * shifted]
                moved = jnp.concatenate([held, rest.astype(high)], axis=0)
            else:
                moved = held
            ends = own_in[part, index * edge:(index + 1) * edge].astype(high)
            low_half, high_half = moved[:edge], moved[edge:]
            new[part, index, :edge] = jnp.where(
                jnp.logical_and(keeps, last), low_half, ends).astype(low)
            new[part, index, edge:2 * edge] = jnp.where(
                keeps, jnp.where(last, high_half, low_half), zero).astype(low)
            new[part, index, 2 * edge:] = jnp.where(
                keeps, jnp.where(last, ends, high_half), zero).astype(low)
            if index == 0:
                if shifted:
                    other = jnp.concatenate([
                        back_in[part, edge:edge + kept].astype(high),
                        slot_in[part, :shifted].astype(high)], axis=0)
                    moved = jnp.where(owns_moved(middle), moved, other)
                placed[part, edge:edge + middle] = moved.astype(low)
                peer_ends = back_in[part, :edge].astype(high)
                placed[part, :edge] = jnp.where(last, peer_ends, ends).astype(low)
                placed[part, edge + middle:] = jnp.where(last, ends, peer_ends).astype(low)
        store_new(part).start()
        store_placed(part).start()

    def back(turn, shifted):
        @pl.when(turn < parts)
        def _():
            arrive(turn, shifted)

        @pl.when(jnp.logical_and(turn > 0, turn <= parts))
        def _():
            place(turn - 1, shifts[shifts.index(shifted) - 1])

    each(parts + 1, back)

    def finish(part, shifted):
        send_edge(part).wait_send()
        send_own(part).wait_send()
        send_slot(part, shifted).wait_send()
        send_back(part, shifted).wait_send()
        store_new(part).wait()
        store_placed(part).wait()

    each(parts, finish)
    each(parts + lag, lambda part, shifted: send_mid(part, shifted).wait_send())


def fused(bit, shifts, counts, partner, gradients, master, first, second):
    flat_count, model = gradients.shape
    capacity = master.shape[0]
    edge = flat_count - capacity
    middle = flat_count - 2 * edge
    width, lag = 512, 2
    parts = model // width
    mid_rows = max(max(middle, 3 * shifted) for shifted in shifts)
    slot_rows = max(3 * max(middle - shifted, shifted) for shifted in shifts)
    back_rows = edge + max(
        max(middle - shifted, 3 * shifted) if shifted else 0 for shifted in shifts)
    low, high = jnp.bfloat16, jnp.float32
    sems, more_sems = (pltpu.SemaphoreType.DMA((count,)) for count in (parts, parts + lag))
    smem = pl.BlockSpec(memory_space=pltpu.SMEM)
    anywhere = pl.BlockSpec(memory_space=pl.ANY)

    def pair(count, rows):
        return [pltpu.VMEM((count, rows, width), low)] * 2

    return pl.pallas_call(
        functools.partial(fused_kernel, bit, shifts, lag),
        out_shape=(
            jax.ShapeDtypeStruct((3, capacity, model), low),
            jax.ShapeDtypeStruct((flat_count, model), low),
        ),
        in_specs=[smem, smem] + [anywhere] * 4,
        out_specs=(anywhere, anywhere),
        scratch_shapes=[
            pltpu.VMEM((parts, flat_count, width), high),
            pltpu.VMEM((parts, 3, capacity, width), high),
        ] + pair(parts, edge) + pair(parts + lag, mid_rows) + pair(parts, 3 * edge)
        + pair(parts, slot_rows) + pair(parts, back_rows) + [
            pltpu.VMEM((parts, 3, capacity, width), low),
            pltpu.VMEM((parts, flat_count, width), low),
            pltpu.SemaphoreType.DMA((4, parts)),
        ] + [sems] * 2 + [more_sems] * 2 + [sems] * 8,
        compiler_params=pltpu.CompilerParams(
            collective_id=bit, has_side_effects=True, vmem_limit_bytes=38 * 1024 * 1024),
        name=f"fused_bit_{bit}",
    )(counts, partner, gradients, master, first, second)


def body_pairs(gradients, master_rows, first_moment, second_moment, shard_rows, move_partner):
    bits = lax.axis_size("ep").bit_length() - 1
    moved, placed = lax.switch(
        chosen_case(move_partner),
        [functools.partial(fused, bit, shifts_of_bit[bit]) for bit in range(bits)],
        shard_rows, move_partner, gradients[0], master_rows[0], first_moment[0], second_moment[0],
    )
    wide = moved.astype(jnp.float32)
    return (wide[0][None], wide[1][None], wide[2][None], placed)


def body(gradients, master_rows, first_moment, second_moment, shard_rows, move_partner):
    groups = lax.axis_size("dp")
    capacity = master_rows.shape[1]
    flat_count = gradients.shape[1]
    dp_index = lax.axis_index("dp")
    ep_index = lax.axis_index("ep")
    partner = move_partner[ep_index]
    counts = shard_rows[ep_index]
    moved_counts = shard_rows[partner]
    starts = jnp.cumsum(counts) - counts
    moved_starts = jnp.cumsum(moved_counts) - moved_counts
    own_slots = jnp.arange(capacity, dtype=jnp.int32)
    live = (own_slots < counts[dp_index])[:, None]
    state = jnp.stack([master_rows[0], first_moment[0], second_moment[0]])
    slots = jnp.arange(groups * capacity, dtype=jnp.int32)
    owners = slots // capacity
    within = slots % capacity
    live_all = (within < counts[owners])[:, None]
    source = jnp.minimum(starts[owners] + within, flat_count - 1)
    packed = jnp.where(live_all, jnp.take(gradients[0], source, axis=0), 0.0)
    summed = lax.psum_scatter(
        packed.astype(jnp.bfloat16), "dp", scatter_dimension=0, tiled=True
    ).astype(jnp.float32)
    grad_own = summed / groups
    stepped = jnp.where(live, jnp.stack(adam_step(grad_own, state[0], state[1], state[2])), 0.0)
    moved = move_new(stepped, partner, ep_index, move_partner)
    updated, first_new, second_new = (moved[0], moved[1], moved[2])
    whole = lax.all_gather(updated.astype(jnp.bfloat16), "dp", axis=0, tiled=True)
    flat_rows = jnp.arange(flat_count, dtype=jnp.int32)
    owner_flat = jnp.sum((flat_rows[:, None] >= moved_starts[None, 1:]).astype(jnp.int32), axis=1)
    position = owner_flat * capacity + flat_rows - moved_starts[owner_flat]
    placed = jnp.take(whole, position, axis=0)
    return (updated[None], first_new[None], second_new[None], placed)


def solution(mesh):
    placed = (
        P("dp", "ep", None),
        P("ep", "dp", None),
        P("ep", "dp", None),
        P("ep", "dp", None),
        P(),
        P(),
    )
    return jax.shard_map(
        body_pairs if mesh.shape["dp"] == 2 else body,
        mesh=mesh,
        in_specs=placed,
        out_specs=(P("ep", "dp", None), P("ep", "dp", None), P("ep", "dp", None), P("ep", None)),
        check_vma=False,
    )
```

```python
import functools

import jax
import jax.numpy as jnp
from jax import lax
from jax.experimental import pallas as pl
from jax.experimental.pallas import tpu as pltpu
from jax.sharding import PartitionSpec as P

beta_one = 0.9
beta_two = 0.95
learn_rate = 0.02
weight_decay = 0.1
epsilon = 1e-08
shifts_of_bit = ((0,), (16, 32), (16, 32), (32,))
correct_one = 1.0 - 0.9**10
correct_two = 1.0 - 0.95**10


def swapped(array, axis, apart):
    return lax.ppermute(array, axis, [(i, i ^ 1 << apart) for i in range(lax.axis_size(axis))])


def adam_step(grad_rows, weights, first, second):
    first_new = beta_one * first + (1.0 - beta_one) * grad_rows
    second_new = beta_two * second + (1.0 - beta_two) * grad_rows * grad_rows
    ratio = first_new / correct_one / (jnp.sqrt(second_new / correct_two) + epsilon)
    updated = weights - learn_rate * (ratio + weight_decay * weights)
    return updated, first_new, second_new


def chosen_case(move_partner):
    count = move_partner.shape[0]
    flips = jnp.bitwise_xor(move_partner, jnp.arange(count, dtype=jnp.int32))
    digit = jnp.max(flips)
    return sum((digit >= 1 << bit).astype(jnp.int32) for bit in range(1, count.bit_length() - 1))


def move_new(values, partner, ep_index, move_partner):
    bits = lax.axis_size("ep").bit_length() - 1

    def exchange(bit_index):
        def run(values):
            arrived = swapped(values.astype(jnp.bfloat16), "ep", bit_index)
            return jnp.where(partner == ep_index, values, arrived.astype(values.dtype))
        return run

    return lax.switch(
        chosen_case(move_partner), [exchange(bit_index) for bit_index in range(bits)], values
    )


def fused_kernel(
    bit, shifts, lag, counts_ref, partner_ref, grad_hbm, master_hbm, first_hbm, second_hbm,
    new_hbm, placed_hbm,
    grad, state, edge_out, edge_in, mid_out, mid_in, own_out, own_in, slot_out, slot_in,
    back_out, back_in, new, placed,
    load_sem, edge_send, edge_recv, mid_send, mid_recv, own_send, own_recv,
    slot_send, slot_recv, back_send, back_recv, new_sem, placed_sem,
):
    parts, flat_count, width = grad.shape
    capacity = state.shape[2]
    edge = flat_count - capacity
    middle = flat_count - 2 * edge
    ahead, trail = 4, 4
    low, high = jnp.bfloat16, jnp.float32
    ep_index, dp_index = lax.axis_index("ep"), lax.axis_index("dp")
    step = 1 << bit
    mate = ep_index + step * (1 - 2 * ((ep_index // step) % 2))
    to_peer, to_mate = {"dp": 1 - dp_index}, {"ep": mate}
    mesh_ids = pl.DeviceIdType.MESH

    def columns(part):
        return pl.ds(pl.multiple_of(part * width, width), width)

    def load(part, index):
        source = (grad_hbm, master_hbm, first_hbm, second_hbm)[index]
        target = grad.at[part] if index == 0 else state.at[part, index - 1]
        return pltpu.make_async_copy(
            source.at[:, columns(part)], target, load_sem.at[index, part])

    def remote(part, rows, out, into, sent, received, target):
        return pltpu.make_async_remote_copy(
            out.at[part, :rows], into.at[part, :rows], sent.at[part], received.at[part],
            device_id=target, device_id_type=mesh_ids)

    def send_edge(part):
        return remote(part, edge, edge_out, edge_in, edge_send, edge_recv, to_peer)

    def send_mid(part, shifted):
        rows = max(middle, 3 * shifted)
        return remote(part, rows, mid_out, mid_in, mid_send, mid_recv, to_peer)

    def send_own(part):
        return remote(part, 3 * edge, own_out, own_in, own_send, own_recv, to_mate)

    def send_slot(part, shifted):
        rows = 3 * max(middle - shifted, shifted)
        return remote(part, rows, slot_out, slot_in, slot_send, slot_recv, to_mate)

    def send_back(part, shifted):
        rows = edge + (max(middle - shifted, 3 * shifted) if shifted else 0)
        return remote(part, rows, back_out, back_in, back_send, back_recv, to_peer)

    def store_new(part):
        return pltpu.make_async_copy(new.at[part], new_hbm.at[:, :, columns(part)], new_sem.at[part])

    def store_placed(part):
        return pltpu.make_async_copy(
            placed.at[part], placed_hbm.at[:, columns(part)], placed_sem.at[part])

    def each(count, step_of):
        def run(group, carry):
            for index, shifted in enumerate(shifts):
                step_of(group * len(shifts) + index, shifted)
            return carry
        lax.fori_loop(0, -(-count // len(shifts)), run, 0)

    barrier = pltpu.get_barrier_semaphore()
    pl.semaphore_signal(barrier, inc=1, device_id=to_peer, device_id_type=mesh_ids)
    pl.semaphore_signal(barrier, inc=1, device_id=to_mate, device_id_type=mesh_ids)
    for index in range(4):
        for part in range(ahead):
            load(part, index).start()
    pl.semaphore_wait(barrier, 2)

    source = partner_ref[ep_index]
    owns_value = counts_ref[ep_index, dp_index]
    moves_value = source
    owns_moved_value = counts_ref[source, dp_index]

    def full(value, rows):
        return jnp.broadcast_to(value, (rows, width))

    def owns(rows):
        return full(owns_value, rows) == capacity

    def owns_moved(rows):
        return full(owns_moved_value, rows) == capacity

    def moves(rows):
        return full(moves_value, rows) != ep_index

    def is_last(rows):
        return full(dp_index, rows) == 1

    def select(mask, one, other):
        return jnp.where(mask, one.astype(high), other.astype(high))

    own_edge = pl.ds(pl.multiple_of((flat_count - edge) * dp_index, edge), edge)
    peer_edge = pl.ds(pl.multiple_of((flat_count - edge) * (1 - dp_index), edge), edge)
    own_middle = pl.ds(pl.multiple_of(edge * (1 - dp_index), edge), middle)

    def update_edge(part):
        send_edge(part).wait_recv()
        for index in range(1, 4):
            load(part, index).wait()
        edge_mean = (grad[part, own_edge] + edge_in[part].astype(high)) / 2
        late = jnp.logical_and(owns(edge), is_last(edge))
        edge_state = [
            jnp.where(late, state[part, index, capacity - edge:], state[part, index, :edge])
            for index in range(3)
        ]
        for index, result in enumerate(adam_step(edge_mean, *edge_state)):
            own_out[part, index * edge:(index + 1) * edge] = result.astype(low)
        send_own(part).start()

    def update_middle(part, shifted):
        kept = middle - shifted
        slot_rows = max(kept, shifted)
        middle_mean = (
            grad[part, edge:edge + middle] + mid_in[part, :middle].astype(high)) / 2
        middle_state = [state[part, index, own_middle] for index in range(3)]
        for index, result in enumerate(adam_step(middle_mean, *middle_state)):
            result = result.astype(low)
            slot_out[part, index * slot_rows:index * slot_rows + kept] = result[:kept]
            if shifted:
                mid_out[part + lag, index * shifted:(index + 1) * shifted] = result[kept:]
            elif index == 0:
                mid_out[part + lag, :middle] = result

    def front(turn, shifted):
        @pl.when(turn < parts)
        def _():
            load(turn, 0).wait()
            edge_out[turn] = grad[turn, peer_edge].astype(low)
            send_edge(turn).start()

        @pl.when(turn + ahead < parts)
        def _():
            for index in range(4):
                load(turn + ahead, index).start()

        @pl.when(turn >= lag)
        def _():
            send_mid(turn - lag, shifted).wait_recv()

        @pl.when(jnp.logical_and(turn >= lag, turn < parts + lag))
        def _():
            update_middle(turn - lag, shifted)

        @pl.when(turn < lag)
        def _():
            mid_out[turn, :middle] = grad[turn, edge:edge + middle].astype(low)

        @pl.when(jnp.logical_and(turn >= lag, turn < parts))
        def _():
            mid_out[turn, :middle] = select(
                owns(middle), mid_out[turn, :middle], grad[turn, edge:edge + middle]).astype(low)

        @pl.when(turn < parts + lag)
        def _():
            send_mid(turn, shifted).start()

        @pl.when(jnp.logical_and(turn >= 1, turn < parts + 1))
        def _():
            update_edge(turn - 1)

        @pl.when(turn >= 2 * lag)
        def _():
            part = turn - 2 * lag
            slot_rows = max(middle - shifted, shifted)
            pieces = [(index * slot_rows, index * shifted, shifted) for index in range(3)]
            for at, come, rows in pieces if shifted else [(0, 0, middle)]:
                slot_out[part, at:at + rows] = select(
                    owns(rows), slot_out[part, at:at + rows],
                    mid_in[turn - lag, come:come + rows]).astype(low)
            send_slot(part, shifted).start()

    each(parts + 2 * lag, front)

    def arrive(part, shifted):
        slot_rows = max(middle - shifted, shifted)
        send_own(part).wait_recv()
        own_in[part] = select(moves(3 * edge), own_in[part], own_out[part]).astype(low)
        back_out[part, :edge] = own_in[part, :edge]
        send_slot(part, shifted).wait_recv()
        rows = 3 * slot_rows
        slot_in[part, :rows] = select(
            moves(rows), slot_in[part, :rows], slot_out[part, :rows]).astype(low)
        if shifted:
            for index in range(3):
                at = index * shifted
                back_out[part, edge + at:edge + at + shifted] = select(
                    owns_moved(shifted), slot_in[part, at:at + shifted],
                    slot_in[part, index * slot_rows:index * slot_rows + shifted]).astype(low)
        send_back(part, shifted).start()

    def place(part, shifted):
        kept = middle - shifted
        slot_rows = max(kept, shifted)
        send_back(part, shifted).wait_recv()
        keeps, last = owns_moved(edge), is_last(edge)
        zero = jnp.zeros((edge, width), high)
        for index in range(3):
            held = slot_in[part, index * slot_rows:index * slot_rows + kept].astype(high)
            if shifted:
                rest = back_in[part, edge + index * shifted:edge + (index + 1) * shifted]
                moved = jnp.concatenate([held, rest.astype(high)], axis=0)
            else:
                moved = held
            ends = own_in[part, index * edge:(index + 1) * edge].astype(high)
            low_half, high_half = moved[:edge], moved[edge:]
            new[part, index, :edge] = jnp.where(
                jnp.logical_and(keeps, last), low_half, ends).astype(low)
            new[part, index, edge:2 * edge] = jnp.where(
                keeps, jnp.where(last, high_half, low_half), zero).astype(low)
            new[part, index, 2 * edge:] = jnp.where(
                keeps, jnp.where(last, ends, high_half), zero).astype(low)
            if index == 0:
                if shifted:
                    other = jnp.concatenate([
                        back_in[part, edge:edge + kept].astype(high),
                        slot_in[part, :shifted].astype(high)], axis=0)
                    moved = jnp.where(owns_moved(middle), moved, other)
                placed[part, edge:edge + middle] = moved.astype(low)
                peer_ends = back_in[part, :edge].astype(high)
                placed[part, :edge] = jnp.where(last, peer_ends, ends).astype(low)
                placed[part, edge + middle:] = jnp.where(last, ends, peer_ends).astype(low)
        store_new(part).start()
        store_placed(part).start()

    def finish(part, shifted):
        send_edge(part).wait_send()
        send_mid(part, shifted).wait_send()
        send_own(part).wait_send()
        send_slot(part, shifted).wait_send()
        send_back(part, shifted).wait_send()
        store_new(part).wait()
        store_placed(part).wait()

    def back(turn, shifted):
        @pl.when(turn < parts)
        def _():
            arrive(turn, shifted)

        @pl.when(jnp.logical_and(turn > 0, turn <= parts))
        def _():
            place(turn - 1, shifts[shifts.index(shifted) - 1])

        @pl.when(turn >= trail)
        def _():
            finish(turn - trail, shifted)

    each(parts + trail, back)
    each(lag, lambda part, shifted: send_mid(parts + part, shifted).wait_send())


def fused(bit, shifts, counts, partner, gradients, master, first, second):
    flat_count, model = gradients.shape
    capacity = master.shape[0]
    edge = flat_count - capacity
    middle = flat_count - 2 * edge
    width, lag = 256, 4
    parts = model // width
    mid_rows = max(max(middle, 3 * shifted) for shifted in shifts)
    slot_rows = max(3 * max(middle - shifted, shifted) for shifted in shifts)
    back_rows = edge + max(
        max(middle - shifted, 3 * shifted) if shifted else 0 for shifted in shifts)
    low, high = jnp.bfloat16, jnp.float32
    sems, more_sems = (pltpu.SemaphoreType.DMA((count,)) for count in (parts, parts + lag))
    smem = pl.BlockSpec(memory_space=pltpu.SMEM)
    anywhere = pl.BlockSpec(memory_space=pl.ANY)

    def pair(count, rows):
        return [pltpu.VMEM((count, rows, width), low)] * 2

    return pl.pallas_call(
        functools.partial(fused_kernel, bit, shifts, lag),
        out_shape=(
            jax.ShapeDtypeStruct((3, capacity, model), low),
            jax.ShapeDtypeStruct((flat_count, model), low),
        ),
        in_specs=[smem, smem] + [anywhere] * 4,
        out_specs=(anywhere, anywhere),
        scratch_shapes=[
            pltpu.VMEM((parts, flat_count, width), high),
            pltpu.VMEM((parts, 3, capacity, width), high),
        ] + pair(parts, edge) + pair(parts + lag, mid_rows) + pair(parts, 3 * edge)
        + pair(parts, slot_rows) + pair(parts, back_rows) + [
            pltpu.VMEM((parts, 3, capacity, width), low),
            pltpu.VMEM((parts, flat_count, width), low),
            pltpu.SemaphoreType.DMA((4, parts)),
        ] + [sems] * 2 + [more_sems] * 2 + [sems] * 8,
        compiler_params=pltpu.CompilerParams(
            collective_id=bit, has_side_effects=True, vmem_limit_bytes=38 * 1024 * 1024),
        name=f"fused_bit_{bit}",
    )(counts, partner, gradients, master, first, second)


def body_pairs(gradients, master_rows, first_moment, second_moment, shard_rows, move_partner):
    bits = lax.axis_size("ep").bit_length() - 1
    moved, placed = lax.switch(
        chosen_case(move_partner),
        [functools.partial(fused, bit, shifts_of_bit[bit]) for bit in range(bits)],
        shard_rows, move_partner, gradients[0], master_rows[0], first_moment[0], second_moment[0],
    )
    wide = moved.astype(jnp.float32)
    return (wide[0][None], wide[1][None], wide[2][None], placed)


def body(gradients, master_rows, first_moment, second_moment, shard_rows, move_partner):
    groups = lax.axis_size("dp")
    capacity = master_rows.shape[1]
    flat_count = gradients.shape[1]
    dp_index = lax.axis_index("dp")
    ep_index = lax.axis_index("ep")
    partner = move_partner[ep_index]
    counts = shard_rows[ep_index]
    moved_counts = shard_rows[partner]
    starts = jnp.cumsum(counts) - counts
    moved_starts = jnp.cumsum(moved_counts) - moved_counts
    own_slots = jnp.arange(capacity, dtype=jnp.int32)
    live = (own_slots < counts[dp_index])[:, None]
    state = jnp.stack([master_rows[0], first_moment[0], second_moment[0]])
    slots = jnp.arange(groups * capacity, dtype=jnp.int32)
    owners = slots // capacity
    within = slots % capacity
    live_all = (within < counts[owners])[:, None]
    source = jnp.minimum(starts[owners] + within, flat_count - 1)
    packed = jnp.where(live_all, jnp.take(gradients[0], source, axis=0), 0.0)
    summed = lax.psum_scatter(
        packed.astype(jnp.bfloat16), "dp", scatter_dimension=0, tiled=True
    ).astype(jnp.float32)
    grad_own = summed / groups
    stepped = jnp.where(live, jnp.stack(adam_step(grad_own, state[0], state[1], state[2])), 0.0)
    moved = move_new(stepped, partner, ep_index, move_partner)
    updated, first_new, second_new = (moved[0], moved[1], moved[2])
    whole = lax.all_gather(updated.astype(jnp.bfloat16), "dp", axis=0, tiled=True)
    flat_rows = jnp.arange(flat_count, dtype=jnp.int32)
    owner_flat = jnp.sum((flat_rows[:, None] >= moved_starts[None, 1:]).astype(jnp.int32), axis=1)
    position = owner_flat * capacity + flat_rows - moved_starts[owner_flat]
    placed = jnp.take(whole, position, axis=0)
    return (updated[None], first_new[None], second_new[None], placed)


def solution(mesh):
    placed = (
        P("dp", "ep", None),
        P("ep", "dp", None),
        P("ep", "dp", None),
        P("ep", "dp", None),
        P(),
        P(),
    )
    return jax.shard_map(
        body_pairs if mesh.shape["dp"] == 2 else body,
        mesh=mesh,
        in_specs=placed,
        out_specs=(P("ep", "dp", None), P("ep", "dp", None), P("ep", "dp", None), P("ep", None)),
        check_vma=False,
    )
```

```python
import functools

import jax
import jax.numpy as jnp
from jax import lax
from jax.experimental import pallas as pl
from jax.experimental.pallas import tpu as pltpu
from jax.sharding import PartitionSpec as P

beta_one = 0.9
beta_two = 0.95
learn_rate = 0.02
weight_decay = 0.1
epsilon = 1e-08
shifts_of_bit = ((0,), (16, 32), (16, 32), (32,))
correct_one = 1.0 - 0.9**10
correct_two = 1.0 - 0.95**10


def swapped(array, axis, apart):
    return lax.ppermute(array, axis, [(i, i ^ 1 << apart) for i in range(lax.axis_size(axis))])


def adam_step(grad_rows, weights, first, second):
    first_new = beta_one * first + (1.0 - beta_one) * grad_rows
    second_new = beta_two * second + (1.0 - beta_two) * grad_rows * grad_rows
    ratio = first_new / correct_one / (jnp.sqrt(second_new / correct_two) + epsilon)
    updated = weights - learn_rate * (ratio + weight_decay * weights)
    return updated, first_new, second_new


def chosen_case(move_partner):
    count = move_partner.shape[0]
    flips = jnp.bitwise_xor(move_partner, jnp.arange(count, dtype=jnp.int32))
    digit = jnp.max(flips)
    return sum((digit >= 1 << bit).astype(jnp.int32) for bit in range(1, count.bit_length() - 1))


def move_new(values, partner, ep_index, move_partner):
    bits = lax.axis_size("ep").bit_length() - 1

    def exchange(bit_index):
        def run(values):
            arrived = swapped(values.astype(jnp.bfloat16), "ep", bit_index)
            return jnp.where(partner == ep_index, values, arrived.astype(values.dtype))
        return run

    return lax.switch(
        chosen_case(move_partner), [exchange(bit_index) for bit_index in range(bits)], values
    )


def fused_kernel(
    bit, shifts, lag, counts_ref, partner_ref, grad_hbm, master_hbm, first_hbm, second_hbm,
    new_hbm, placed_hbm,
    grad, state, edge_out, edge_in, mid_out, mid_in, own_out, own_in, slot_out, slot_in,
    back_out, back_in, new, placed,
    load_sem, edge_send, edge_recv, mid_send, mid_recv, own_send, own_recv,
    slot_send, slot_recv, back_send, back_recv, new_sem, placed_sem,
):
    parts, flat_count, width = grad.shape
    capacity = state.shape[2]
    edge = flat_count - capacity
    middle = flat_count - 2 * edge
    ahead, trail = 4, 4
    low, high = jnp.bfloat16, jnp.float32
    ep_index, dp_index = lax.axis_index("ep"), lax.axis_index("dp")
    step = 1 << bit
    mate = ep_index + step * (1 - 2 * ((ep_index // step) % 2))
    to_peer, to_mate = {"dp": 1 - dp_index}, {"ep": mate}
    mesh_ids = pl.DeviceIdType.MESH

    def columns(part):
        return pl.ds(pl.multiple_of(part * width, width), width)

    def load(part, index):
        source = (grad_hbm, master_hbm, first_hbm, second_hbm)[index]
        target = grad.at[part] if index == 0 else state.at[part, index - 1]
        return pltpu.make_async_copy(
            source.at[:, columns(part)], target, load_sem.at[index, part])

    def remote(part, rows, out, into, sent, received, target):
        return pltpu.make_async_remote_copy(
            out.at[part, :rows], into.at[part, :rows], sent.at[part], received.at[part],
            device_id=target, device_id_type=mesh_ids)

    def send_edge(part):
        return remote(part, edge, edge_out, edge_in, edge_send, edge_recv, to_peer)

    def send_mid(part, shifted):
        rows = max(middle, 3 * shifted)
        return remote(part, rows, mid_out, mid_in, mid_send, mid_recv, to_peer)

    def send_own(part):
        return remote(part, 3 * edge, own_out, own_in, own_send, own_recv, to_mate)

    def send_slot(part, shifted):
        rows = 3 * max(middle - shifted, shifted)
        return remote(part, rows, slot_out, slot_in, slot_send, slot_recv, to_mate)

    def send_back(part, shifted):
        rows = edge + (max(middle - shifted, 3 * shifted) if shifted else 0)
        return remote(part, rows, back_out, back_in, back_send, back_recv, to_peer)

    def store_new(part):
        return pltpu.make_async_copy(new.at[part], new_hbm.at[:, :, columns(part)], new_sem.at[part])

    def store_placed(part):
        return pltpu.make_async_copy(
            placed.at[part], placed_hbm.at[:, columns(part)], placed_sem.at[part])

    def each(count, step_of):
        def run(group, carry):
            for index, shifted in enumerate(shifts):
                step_of(group * len(shifts) + index, shifted)
            return carry
        lax.fori_loop(0, -(-count // len(shifts)), run, 0)

    barrier = pltpu.get_barrier_semaphore()
    pl.semaphore_signal(barrier, inc=1, device_id=to_peer, device_id_type=mesh_ids)
    pl.semaphore_signal(barrier, inc=1, device_id=to_mate, device_id_type=mesh_ids)
    for index in range(4):
        for part in range(ahead):
            load(part, index).start()
    pl.semaphore_wait(barrier, 2)

    source = partner_ref[ep_index]
    owns_value = counts_ref[ep_index, dp_index]
    moves_value = source
    owns_moved_value = counts_ref[source, dp_index]

    def full(value, rows):
        return jnp.broadcast_to(value, (rows, width))

    def owns(rows):
        return full(owns_value, rows) == capacity

    def owns_moved(rows):
        return full(owns_moved_value, rows) == capacity

    def moves(rows):
        return full(moves_value, rows) != ep_index

    def is_last(rows):
        return full(dp_index, rows) == 1

    def select(mask, one, other):
        return jnp.where(mask, one.astype(high), other.astype(high))

    own_edge = pl.ds(pl.multiple_of((flat_count - edge) * dp_index, edge), edge)
    peer_edge = pl.ds(pl.multiple_of((flat_count - edge) * (1 - dp_index), edge), edge)
    own_middle = pl.ds(pl.multiple_of(edge * (1 - dp_index), edge), middle)

    def update_edge(part):
        send_edge(part).wait_recv()
        for index in range(1, 4):
            load(part, index).wait()
        edge_mean = (grad[part, own_edge] + edge_in[part].astype(high)) / 2
        late = jnp.logical_and(owns(edge), is_last(edge))
        edge_state = [
            jnp.where(late, state[part, index, capacity - edge:], state[part, index, :edge])
            for index in range(3)
        ]
        for index, result in enumerate(adam_step(edge_mean, *edge_state)):
            own_out[part, index * edge:(index + 1) * edge] = result.astype(low)
        send_own(part).start()

    def update_middle(part, shifted):
        kept = middle - shifted
        slot_rows = max(kept, shifted)
        middle_mean = (
            grad[part, edge:edge + middle] + mid_in[part, :middle].astype(high)) / 2
        middle_state = [state[part, index, own_middle] for index in range(3)]
        for index, result in enumerate(adam_step(middle_mean, *middle_state)):
            result = result.astype(low)
            slot_out[part, index * slot_rows:index * slot_rows + kept] = result[:kept]
            if shifted:
                mid_out[part + lag, index * shifted:(index + 1) * shifted] = result[kept:]
            elif index == 0:
                mid_out[part + lag, :middle] = result

    def front(turn, shifted):
        @pl.when(turn < parts)
        def _():
            load(turn, 0).wait()
            edge_out[turn] = grad[turn, peer_edge].astype(low)
            send_edge(turn).start()

        @pl.when(turn + ahead < parts)
        def _():
            for index in range(4):
                load(turn + ahead, index).start()

        @pl.when(turn >= lag)
        def _():
            send_mid(turn - lag, shifted).wait_recv()

        @pl.when(jnp.logical_and(turn >= lag, turn < parts + lag))
        def _():
            update_middle(turn - lag, shifted)

        @pl.when(turn < lag)
        def _():
            mid_out[turn, :middle] = grad[turn, edge:edge + middle].astype(low)

        @pl.when(jnp.logical_and(turn >= lag, turn < parts))
        def _():
            mid_out[turn, :middle] = select(
                owns(middle), mid_out[turn, :middle], grad[turn, edge:edge + middle]).astype(low)

        @pl.when(turn < parts + lag)
        def _():
            send_mid(turn, shifted).start()

        @pl.when(jnp.logical_and(turn >= 1, turn < parts + 1))
        def _():
            update_edge(turn - 1)

        @pl.when(turn >= 2 * lag)
        def _():
            part = turn - 2 * lag
            slot_rows = max(middle - shifted, shifted)
            pieces = [(index * slot_rows, index * shifted, shifted) for index in range(3)]
            for at, come, rows in pieces if shifted else [(0, 0, middle)]:
                slot_out[part, at:at + rows] = select(
                    owns(rows), slot_out[part, at:at + rows],
                    mid_in[turn - lag, come:come + rows]).astype(low)
            send_slot(part, shifted).start()

    each(parts + 2 * lag, front)

    def arrive(part, shifted):
        slot_rows = max(middle - shifted, shifted)
        send_own(part).wait_recv()
        own_in[part] = select(moves(3 * edge), own_in[part], own_out[part]).astype(low)
        back_out[part, :edge] = own_in[part, :edge]
        send_slot(part, shifted).wait_recv()
        rows = 3 * slot_rows
        slot_in[part, :rows] = select(
            moves(rows), slot_in[part, :rows], slot_out[part, :rows]).astype(low)
        if shifted:
            for index in range(3):
                at = index * shifted
                back_out[part, edge + at:edge + at + shifted] = select(
                    owns_moved(shifted), slot_in[part, at:at + shifted],
                    slot_in[part, index * slot_rows:index * slot_rows + shifted]).astype(low)
        send_back(part, shifted).start()

    def place(part, shifted):
        kept = middle - shifted
        slot_rows = max(kept, shifted)
        send_back(part, shifted).wait_recv()
        keeps, last = owns_moved(edge), is_last(edge)
        zero = jnp.zeros((edge, width), high)
        for index in range(3):
            held = slot_in[part, index * slot_rows:index * slot_rows + kept].astype(high)
            if shifted:
                rest = back_in[part, edge + index * shifted:edge + (index + 1) * shifted]
                moved = jnp.concatenate([held, rest.astype(high)], axis=0)
            else:
                moved = held
            ends = own_in[part, index * edge:(index + 1) * edge].astype(high)
            low_half, high_half = moved[:edge], moved[edge:]
            new[part, index, :edge] = jnp.where(
                jnp.logical_and(keeps, last), low_half, ends).astype(low)
            new[part, index, edge:2 * edge] = jnp.where(
                keeps, jnp.where(last, high_half, low_half), zero).astype(low)
            new[part, index, 2 * edge:] = jnp.where(
                keeps, jnp.where(last, ends, high_half), zero).astype(low)
            if index == 0:
                if shifted:
                    other = jnp.concatenate([
                        back_in[part, edge:edge + kept].astype(high),
                        slot_in[part, :shifted].astype(high)], axis=0)
                    moved = jnp.where(owns_moved(middle), moved, other)
                placed[part, edge:edge + middle] = moved.astype(low)
                peer_ends = back_in[part, :edge].astype(high)
                placed[part, :edge] = jnp.where(last, peer_ends, ends).astype(low)
                placed[part, edge + middle:] = jnp.where(last, ends, peer_ends).astype(low)
        store_new(part).start()
        store_placed(part).start()

    def finish(part, shifted):
        send_edge(part).wait_send()
        send_mid(part, shifted).wait_send()
        send_own(part).wait_send()
        send_slot(part, shifted).wait_send()
        send_back(part, shifted).wait_send()
        store_new(part).wait()
        store_placed(part).wait()

    def back(turn, shifted):
        @pl.when(turn < parts)
        def _():
            arrive(turn, shifted)

        @pl.when(jnp.logical_and(turn > 0, turn <= parts))
        def _():
            place(turn - 1, shifts[shifts.index(shifted) - 1])

        @pl.when(turn >= trail)
        def _():
            finish(turn - trail, shifted)

    each(parts + trail, back)
    each(lag, lambda part, shifted: send_mid(parts + part, shifted).wait_send())


def fused(bit, shifts, counts, partner, gradients, master, first, second):
    flat_count, model = gradients.shape
    capacity = master.shape[0]
    edge = flat_count - capacity
    middle = flat_count - 2 * edge
    width, lag = 512, 2
    parts = model // width
    mid_rows = max(max(middle, 3 * shifted) for shifted in shifts)
    slot_rows = max(3 * max(middle - shifted, shifted) for shifted in shifts)
    back_rows = edge + max(
        max(middle - shifted, 3 * shifted) if shifted else 0 for shifted in shifts)
    low, high = jnp.bfloat16, jnp.float32
    sems, more_sems = (pltpu.SemaphoreType.DMA((count,)) for count in (parts, parts + lag))
    smem = pl.BlockSpec(memory_space=pltpu.SMEM)
    anywhere = pl.BlockSpec(memory_space=pl.ANY)

    def pair(count, rows):
        return [pltpu.VMEM((count, rows, width), low)] * 2

    return pl.pallas_call(
        functools.partial(fused_kernel, bit, shifts, lag),
        out_shape=(
            jax.ShapeDtypeStruct((3, capacity, model), low),
            jax.ShapeDtypeStruct((flat_count, model), low),
        ),
        in_specs=[smem, smem] + [anywhere] * 4,
        out_specs=(anywhere, anywhere),
        scratch_shapes=[
            pltpu.VMEM((parts, flat_count, width), high),
            pltpu.VMEM((parts, 3, capacity, width), high),
        ] + pair(parts, edge) + pair(parts + lag, mid_rows) + pair(parts, 3 * edge)
        + pair(parts, slot_rows) + pair(parts, back_rows) + [
            pltpu.VMEM((parts, 3, capacity, width), low),
            pltpu.VMEM((parts, flat_count, width), low),
            pltpu.SemaphoreType.DMA((4, parts)),
        ] + [sems] * 2 + [more_sems] * 2 + [sems] * 8,
        compiler_params=pltpu.CompilerParams(
            collective_id=bit, has_side_effects=True, vmem_limit_bytes=38 * 1024 * 1024),
        name=f"fused_bit_{bit}",
    )(counts, partner, gradients, master, first, second)


def body_pairs(gradients, master_rows, first_moment, second_moment, shard_rows, move_partner):
    bits = lax.axis_size("ep").bit_length() - 1
    moved, placed = lax.switch(
        chosen_case(move_partner),
        [functools.partial(fused, bit, shifts_of_bit[bit]) for bit in range(bits)],
        shard_rows, move_partner, gradients[0], master_rows[0], first_moment[0], second_moment[0],
    )
    wide = moved.astype(jnp.float32)
    return (wide[0][None], wide[1][None], wide[2][None], placed)


def body(gradients, master_rows, first_moment, second_moment, shard_rows, move_partner):
    groups = lax.axis_size("dp")
    capacity = master_rows.shape[1]
    flat_count = gradients.shape[1]
    dp_index = lax.axis_index("dp")
    ep_index = lax.axis_index("ep")
    partner = move_partner[ep_index]
    counts = shard_rows[ep_index]
    moved_counts = shard_rows[partner]
    starts = jnp.cumsum(counts) - counts
    moved_starts = jnp.cumsum(moved_counts) - moved_counts
    own_slots = jnp.arange(capacity, dtype=jnp.int32)
    live = (own_slots < counts[dp_index])[:, None]
    state = jnp.stack([master_rows[0], first_moment[0], second_moment[0]])
    slots = jnp.arange(groups * capacity, dtype=jnp.int32)
    owners = slots // capacity
    within = slots % capacity
    live_all = (within < counts[owners])[:, None]
    source = jnp.minimum(starts[owners] + within, flat_count - 1)
    packed = jnp.where(live_all, jnp.take(gradients[0], source, axis=0), 0.0)
    summed = lax.psum_scatter(
        packed.astype(jnp.bfloat16), "dp", scatter_dimension=0, tiled=True
    ).astype(jnp.float32)
    grad_own = summed / groups
    stepped = jnp.where(live, jnp.stack(adam_step(grad_own, state[0], state[1], state[2])), 0.0)
    moved = move_new(stepped, partner, ep_index, move_partner)
    updated, first_new, second_new = (moved[0], moved[1], moved[2])
    whole = lax.all_gather(updated.astype(jnp.bfloat16), "dp", axis=0, tiled=True)
    flat_rows = jnp.arange(flat_count, dtype=jnp.int32)
    owner_flat = jnp.sum((flat_rows[:, None] >= moved_starts[None, 1:]).astype(jnp.int32), axis=1)
    position = owner_flat * capacity + flat_rows - moved_starts[owner_flat]
    placed = jnp.take(whole, position, axis=0)
    return (updated[None], first_new[None], second_new[None], placed)


def solution(mesh):
    placed = (
        P("dp", "ep", None),
        P("ep", "dp", None),
        P("ep", "dp", None),
        P("ep", "dp", None),
        P(),
        P(),
    )
    return jax.shard_map(
        body_pairs if mesh.shape["dp"] == 2 else body,
        mesh=mesh,
        in_specs=placed,
        out_specs=(P("ep", "dp", None), P("ep", "dp", None), P("ep", "dp", None), P("ep", None)),
        check_vma=False,
    )
```

```python
import functools

import jax
import jax.numpy as jnp
from jax import lax
from jax.experimental import pallas as pl
from jax.experimental.pallas import tpu as pltpu
from jax.sharding import PartitionSpec as P

beta_one = 0.9
beta_two = 0.95
learn_rate = 0.02
weight_decay = 0.1
epsilon = 1e-08
shifts_of_bit = ((0,), (16, 32), (16, 32), (32,))
correct_one = 1.0 - 0.9**10
correct_two = 1.0 - 0.95**10


def swapped(array, axis, apart):
    return lax.ppermute(array, axis, [(i, i ^ 1 << apart) for i in range(lax.axis_size(axis))])


def adam_step(grad_rows, weights, first, second):
    first_new = beta_one * first + (1.0 - beta_one) * grad_rows
    second_new = beta_two * second + (1.0 - beta_two) * grad_rows * grad_rows
    ratio = first_new / correct_one / (jnp.sqrt(second_new / correct_two) + epsilon)
    updated = weights - learn_rate * (ratio + weight_decay * weights)
    return updated, first_new, second_new


def chosen_case(move_partner):
    count = move_partner.shape[0]
    flips = jnp.bitwise_xor(move_partner, jnp.arange(count, dtype=jnp.int32))
    digit = jnp.max(flips)
    return sum((digit >= 1 << bit).astype(jnp.int32) for bit in range(1, count.bit_length() - 1))


def move_new(values, partner, ep_index, move_partner):
    bits = lax.axis_size("ep").bit_length() - 1

    def exchange(bit_index):
        def run(values):
            arrived = swapped(values.astype(jnp.bfloat16), "ep", bit_index)
            return jnp.where(partner == ep_index, values, arrived.astype(values.dtype))
        return run

    return lax.switch(
        chosen_case(move_partner), [exchange(bit_index) for bit_index in range(bits)], values
    )


def fused_kernel(
    bit, shifts, lag, counts_ref, partner_ref, grad_hbm, master_hbm, first_hbm, second_hbm,
    new_hbm, placed_hbm,
    grad, state, edge_out, edge_in, mid_out, mid_in, own_out, own_in, slot_out, slot_in,
    back_out, back_in, new, placed,
    load_sem, edge_send, edge_recv, mid_send, mid_recv, own_send, own_recv, rest_send, rest_recv,
    slot_send, slot_recv, back_send, back_recv, new_sem, placed_sem,
):
    parts, flat_count, width = grad.shape
    capacity = state.shape[2]
    edge = flat_count - capacity
    middle = flat_count - 2 * edge
    ahead, trail = 4, 4
    deferred = parts - (6 if bit else 0)
    low, high = jnp.bfloat16, jnp.float32
    ep_index, dp_index = lax.axis_index("ep"), lax.axis_index("dp")
    step = 1 << bit
    mate = ep_index + step * (1 - 2 * ((ep_index // step) % 2))
    to_peer, to_mate = {"dp": 1 - dp_index}, {"ep": mate}
    mesh_ids = pl.DeviceIdType.MESH

    def columns(part):
        return pl.ds(pl.multiple_of(part * width, width), width)

    def load(part, index):
        source = (grad_hbm, master_hbm, first_hbm, second_hbm)[index]
        target = grad.at[part] if index == 0 else state.at[part, index - 1]
        return pltpu.make_async_copy(
            source.at[:, columns(part)], target, load_sem.at[index, part])

    def remote(part, rows, out, into, sent, received, target):
        return pltpu.make_async_remote_copy(
            out.at[part, :rows], into.at[part, :rows], sent.at[part], received.at[part],
            device_id=target, device_id_type=mesh_ids)

    def send_edge(part):
        return remote(part, edge, edge_out, edge_in, edge_send, edge_recv, to_peer)

    def send_mid(part, shifted):
        rows = max(middle, 3 * shifted)
        return remote(part, rows, mid_out, mid_in, mid_send, mid_recv, to_peer)

    def send_own(part, rows):
        return remote(part, rows, own_out, own_in, own_send, own_recv, to_mate)

    def send_rest(part):
        return pltpu.make_async_remote_copy(
            own_out.at[part, edge:], own_in.at[part, edge:], rest_send.at[part],
            rest_recv.at[part], device_id=to_mate, device_id_type=mesh_ids)

    def either(part, step_of):
        @pl.when(part < deferred)
        def _():
            step_of(3 * edge)

        @pl.when(part >= deferred)
        def _():
            step_of(edge)

    def send_slot(part, shifted):
        rows = 3 * max(middle - shifted, shifted)
        return remote(part, rows, slot_out, slot_in, slot_send, slot_recv, to_mate)

    def send_back(part, shifted):
        rows = edge + (max(middle - shifted, 3 * shifted) if shifted else 0)
        return remote(part, rows, back_out, back_in, back_send, back_recv, to_peer)

    def store_new(part):
        return pltpu.make_async_copy(new.at[part], new_hbm.at[:, :, columns(part)], new_sem.at[part])

    def store_placed(part):
        return pltpu.make_async_copy(
            placed.at[part], placed_hbm.at[:, columns(part)], placed_sem.at[part])

    def each(count, step_of):
        def run(group, carry):
            for index, shifted in enumerate(shifts):
                step_of(group * len(shifts) + index, shifted)
            return carry
        lax.fori_loop(0, -(-count // len(shifts)), run, 0)

    barrier = pltpu.get_barrier_semaphore()
    pl.semaphore_signal(barrier, inc=1, device_id=to_peer, device_id_type=mesh_ids)
    pl.semaphore_signal(barrier, inc=1, device_id=to_mate, device_id_type=mesh_ids)
    for index in range(4):
        for part in range(ahead):
            load(part, index).start()
    pl.semaphore_wait(barrier, 2)

    source = partner_ref[ep_index]
    owns_value = counts_ref[ep_index, dp_index]
    moves_value = source
    owns_moved_value = counts_ref[source, dp_index]

    def full(value, rows):
        return jnp.broadcast_to(value, (rows, width))

    def owns(rows):
        return full(owns_value, rows) == capacity

    def owns_moved(rows):
        return full(owns_moved_value, rows) == capacity

    def moves(rows):
        return full(moves_value, rows) != ep_index

    def is_last(rows):
        return full(dp_index, rows) == 1

    def select(mask, one, other):
        return jnp.where(mask, one.astype(high), other.astype(high))

    own_edge = pl.ds(pl.multiple_of((flat_count - edge) * dp_index, edge), edge)
    peer_edge = pl.ds(pl.multiple_of((flat_count - edge) * (1 - dp_index), edge), edge)
    own_middle = pl.ds(pl.multiple_of(edge * (1 - dp_index), edge), middle)

    def update_edge(part):
        send_edge(part).wait_recv()
        for index in range(1, 4):
            load(part, index).wait()
        edge_mean = (grad[part, own_edge] + edge_in[part].astype(high)) / 2
        late = jnp.logical_and(owns(edge), is_last(edge))
        edge_state = [
            jnp.where(late, state[part, index, capacity - edge:], state[part, index, :edge])
            for index in range(3)
        ]
        for index, result in enumerate(adam_step(edge_mean, *edge_state)):
            own_out[part, index * edge:(index + 1) * edge] = result.astype(low)
        either(part, lambda rows: send_own(part, rows).start())

    def update_middle(part, shifted):
        kept = middle - shifted
        slot_rows = max(kept, shifted)
        middle_mean = (
            grad[part, edge:edge + middle] + mid_in[part, :middle].astype(high)) / 2
        middle_state = [state[part, index, own_middle] for index in range(3)]
        for index, result in enumerate(adam_step(middle_mean, *middle_state)):
            result = result.astype(low)
            slot_out[part, index * slot_rows:index * slot_rows + kept] = result[:kept]
            if shifted:
                mid_out[part + lag, index * shifted:(index + 1) * shifted] = result[kept:]
            elif index == 0:
                mid_out[part + lag, :middle] = result

    def front(turn, shifted):
        @pl.when(turn < parts)
        def _():
            load(turn, 0).wait()
            edge_out[turn] = grad[turn, peer_edge].astype(low)
            send_edge(turn).start()

        @pl.when(turn + ahead < parts)
        def _():
            for index in range(4):
                load(turn + ahead, index).start()

        @pl.when(turn >= lag)
        def _():
            send_mid(turn - lag, shifted).wait_recv()

        @pl.when(jnp.logical_and(turn >= lag, turn < parts + lag))
        def _():
            update_middle(turn - lag, shifted)

        @pl.when(turn < lag)
        def _():
            mid_out[turn, :middle] = grad[turn, edge:edge + middle].astype(low)

        @pl.when(jnp.logical_and(turn >= lag, turn < parts))
        def _():
            mid_out[turn, :middle] = select(
                owns(middle), mid_out[turn, :middle], grad[turn, edge:edge + middle]).astype(low)

        @pl.when(turn < parts + lag)
        def _():
            send_mid(turn, shifted).start()

        @pl.when(jnp.logical_and(turn >= 1, turn < parts + 1))
        def _():
            update_edge(turn - 1)

        @pl.when(turn >= 2 * lag)
        def _():
            part = turn - 2 * lag
            slot_rows = max(middle - shifted, shifted)
            pieces = [(index * slot_rows, index * shifted, shifted) for index in range(3)]
            for at, come, rows in pieces if shifted else [(0, 0, middle)]:
                slot_out[part, at:at + rows] = select(
                    owns(rows), slot_out[part, at:at + rows],
                    mid_in[turn - lag, come:come + rows]).astype(low)
            send_slot(part, shifted).start()

    each(parts + 2 * lag, front)

    def later(step_of):
        def run(part, carry):
            step_of(part)
            return carry
        lax.fori_loop(deferred, parts, run, 0)

    later(lambda part: send_rest(part).start())

    def arrive(part, shifted):
        slot_rows = max(middle - shifted, shifted)
        def take(rows):
            send_own(part, rows).wait_recv()
            own_in[part, :rows] = select(
                moves(rows), own_in[part, :rows], own_out[part, :rows]).astype(low)

        either(part, take)
        back_out[part, :edge] = own_in[part, :edge]
        send_slot(part, shifted).wait_recv()
        rows = 3 * slot_rows
        slot_in[part, :rows] = select(
            moves(rows), slot_in[part, :rows], slot_out[part, :rows]).astype(low)
        if shifted:
            for index in range(3):
                at = index * shifted
                back_out[part, edge + at:edge + at + shifted] = select(
                    owns_moved(shifted), slot_in[part, at:at + shifted],
                    slot_in[part, index * slot_rows:index * slot_rows + shifted]).astype(low)
        send_back(part, shifted).start()

    def place(part, shifted):
        either(part, functools.partial(place_with, part, shifted))

    def place_with(part, shifted, ready):
        kept = middle - shifted
        slot_rows = max(kept, shifted)
        send_back(part, shifted).wait_recv()
        keeps, last = owns_moved(edge), is_last(edge)
        zero = jnp.zeros((edge, width), high)
        for index in range(3):
            held = slot_in[part, index * slot_rows:index * slot_rows + kept].astype(high)
            if shifted:
                rest = back_in[part, edge + index * shifted:edge + (index + 1) * shifted]
                moved = jnp.concatenate([held, rest.astype(high)], axis=0)
            else:
                moved = held
            ends = zero
            if index * edge < ready:
                ends = own_in[part, index * edge:(index + 1) * edge].astype(high)
            low_half, high_half = moved[:edge], moved[edge:]
            new[part, index, :edge] = jnp.where(
                jnp.logical_and(keeps, last), low_half, ends).astype(low)
            new[part, index, edge:2 * edge] = jnp.where(
                keeps, jnp.where(last, high_half, low_half), zero).astype(low)
            new[part, index, 2 * edge:] = jnp.where(
                keeps, jnp.where(last, ends, high_half), zero).astype(low)
            if index == 0:
                if shifted:
                    other = jnp.concatenate([
                        back_in[part, edge:edge + kept].astype(high),
                        slot_in[part, :shifted].astype(high)], axis=0)
                    moved = jnp.where(owns_moved(middle), moved, other)
                placed[part, edge:edge + middle] = moved.astype(low)
                peer_ends = back_in[part, :edge].astype(high)
                placed[part, :edge] = jnp.where(last, peer_ends, ends).astype(low)
                placed[part, edge + middle:] = jnp.where(last, ends, peer_ends).astype(low)
        if ready > edge:
            store_new(part).start()
        store_placed(part).start()

    def place_rest(part):
        send_rest(part).wait_recv()
        late = jnp.logical_and(owns_moved(edge), is_last(edge))
        for index in (1, 2):
            rows = slice(index * edge, (index + 1) * edge)
            ends = select(moves(edge), own_in[part, rows], own_out[part, rows])
            new[part, index, :edge] = select(late, new[part, index, :edge], ends).astype(low)
            new[part, index, 2 * edge:] = select(
                late, ends, new[part, index, 2 * edge:]).astype(low)
        store_new(part).start()

    def finish(part, shifted):
        send_edge(part).wait_send()
        send_mid(part, shifted).wait_send()
        either(part, lambda rows: send_own(part, rows).wait_send())
        send_slot(part, shifted).wait_send()
        send_back(part, shifted).wait_send()
        store_placed(part).wait()

        @pl.when(part < deferred)
        def _():
            store_new(part).wait()

    def back(turn, shifted):
        @pl.when(turn < parts)
        def _():
            arrive(turn, shifted)

        @pl.when(jnp.logical_and(turn > 0, turn <= parts))
        def _():
            place(turn - 1, shifts[shifts.index(shifted) - 1])

        @pl.when(turn >= trail)
        def _():
            finish(turn - trail, shifted)

    each(parts + trail, back)
    each(lag, lambda part, shifted: send_mid(parts + part, shifted).wait_send())
    later(place_rest)

    def finish_rest(part):
        send_rest(part).wait_send()
        store_new(part).wait()

    later(finish_rest)


def fused(bit, shifts, counts, partner, gradients, master, first, second):
    flat_count, model = gradients.shape
    capacity = master.shape[0]
    edge = flat_count - capacity
    middle = flat_count - 2 * edge
    width, lag = 512, 2
    parts = model // width
    mid_rows = max(max(middle, 3 * shifted) for shifted in shifts)
    slot_rows = max(3 * max(middle - shifted, shifted) for shifted in shifts)
    back_rows = edge + max(
        max(middle - shifted, 3 * shifted) if shifted else 0 for shifted in shifts)
    low, high = jnp.bfloat16, jnp.float32
    sems, more_sems = (pltpu.SemaphoreType.DMA((count,)) for count in (parts, parts + lag))
    smem = pl.BlockSpec(memory_space=pltpu.SMEM)
    anywhere = pl.BlockSpec(memory_space=pl.ANY)

    def pair(count, rows):
        return [pltpu.VMEM((count, rows, width), low)] * 2

    return pl.pallas_call(
        functools.partial(fused_kernel, bit, shifts, lag),
        out_shape=(
            jax.ShapeDtypeStruct((3, capacity, model), low),
            jax.ShapeDtypeStruct((flat_count, model), low),
        ),
        in_specs=[smem, smem] + [anywhere] * 4,
        out_specs=(anywhere, anywhere),
        scratch_shapes=[
            pltpu.VMEM((parts, flat_count, width), high),
            pltpu.VMEM((parts, 3, capacity, width), high),
        ] + pair(parts, edge) + pair(parts + lag, mid_rows) + pair(parts, 3 * edge)
        + pair(parts, slot_rows) + pair(parts, back_rows) + [
            pltpu.VMEM((parts, 3, capacity, width), low),
            pltpu.VMEM((parts, flat_count, width), low),
            pltpu.SemaphoreType.DMA((4, parts)),
        ] + [sems] * 2 + [more_sems] * 2 + [sems] * 10,
        compiler_params=pltpu.CompilerParams(
            collective_id=bit, has_side_effects=True, vmem_limit_bytes=38 * 1024 * 1024),
        name=f"fused_bit_{bit}",
    )(counts, partner, gradients, master, first, second)


def body_pairs(gradients, master_rows, first_moment, second_moment, shard_rows, move_partner):
    bits = lax.axis_size("ep").bit_length() - 1
    moved, placed = lax.switch(
        chosen_case(move_partner),
        [functools.partial(fused, bit, shifts_of_bit[bit]) for bit in range(bits)],
        shard_rows, move_partner, gradients[0], master_rows[0], first_moment[0], second_moment[0],
    )
    wide = moved.astype(jnp.float32)
    return (wide[0][None], wide[1][None], wide[2][None], placed)


def body(gradients, master_rows, first_moment, second_moment, shard_rows, move_partner):
    groups = lax.axis_size("dp")
    capacity = master_rows.shape[1]
    flat_count = gradients.shape[1]
    dp_index = lax.axis_index("dp")
    ep_index = lax.axis_index("ep")
    partner = move_partner[ep_index]
    counts = shard_rows[ep_index]
    moved_counts = shard_rows[partner]
    starts = jnp.cumsum(counts) - counts
    moved_starts = jnp.cumsum(moved_counts) - moved_counts
    own_slots = jnp.arange(capacity, dtype=jnp.int32)
    live = (own_slots < counts[dp_index])[:, None]
    state = jnp.stack([master_rows[0], first_moment[0], second_moment[0]])
    slots = jnp.arange(groups * capacity, dtype=jnp.int32)
    owners = slots // capacity
    within = slots % capacity
    live_all = (within < counts[owners])[:, None]
    source = jnp.minimum(starts[owners] + within, flat_count - 1)
    packed = jnp.where(live_all, jnp.take(gradients[0], source, axis=0), 0.0)
    summed = lax.psum_scatter(
        packed.astype(jnp.bfloat16), "dp", scatter_dimension=0, tiled=True
    ).astype(jnp.float32)
    grad_own = summed / groups
    stepped = jnp.where(live, jnp.stack(adam_step(grad_own, state[0], state[1], state[2])), 0.0)
    moved = move_new(stepped, partner, ep_index, move_partner)
    updated, first_new, second_new = (moved[0], moved[1], moved[2])
    whole = lax.all_gather(updated.astype(jnp.bfloat16), "dp", axis=0, tiled=True)
    flat_rows = jnp.arange(flat_count, dtype=jnp.int32)
    owner_flat = jnp.sum((flat_rows[:, None] >= moved_starts[None, 1:]).astype(jnp.int32), axis=1)
    position = owner_flat * capacity + flat_rows - moved_starts[owner_flat]
    placed = jnp.take(whole, position, axis=0)
    return (updated[None], first_new[None], second_new[None], placed)


def solution(mesh):
    placed = (
        P("dp", "ep", None),
        P("ep", "dp", None),
        P("ep", "dp", None),
        P("ep", "dp", None),
        P(),
        P(),
    )
    return jax.shard_map(
        body_pairs if mesh.shape["dp"] == 2 else body,
        mesh=mesh,
        in_specs=placed,
        out_specs=(P("ep", "dp", None), P("ep", "dp", None), P("ep", "dp", None), P("ep", None)),
        check_vma=False,
    )
```

```python
import functools

import jax
import jax.numpy as jnp
from jax import lax
from jax.experimental import pallas as pl
from jax.experimental.pallas import tpu as pltpu
from jax.sharding import PartitionSpec as P

beta_one = 0.9
beta_two = 0.95
learn_rate = 0.02
weight_decay = 0.1
epsilon = 1e-08
shifts_of_bit = ((0,), (16, 32), (16, 32), (32,))
correct_one = 1.0 - 0.9**10
correct_two = 1.0 - 0.95**10


def swapped(array, axis, apart):
    return lax.ppermute(array, axis, [(i, i ^ 1 << apart) for i in range(lax.axis_size(axis))])


def adam_step(grad_rows, weights, first, second):
    first_new = beta_one * first + (1.0 - beta_one) * grad_rows
    second_new = beta_two * second + (1.0 - beta_two) * grad_rows * grad_rows
    ratio = first_new / correct_one / (jnp.sqrt(second_new / correct_two) + epsilon)
    updated = weights - learn_rate * (ratio + weight_decay * weights)
    return updated, first_new, second_new


def chosen_case(move_partner):
    count = move_partner.shape[0]
    flips = jnp.bitwise_xor(move_partner, jnp.arange(count, dtype=jnp.int32))
    digit = jnp.max(flips)
    return sum((digit >= 1 << bit).astype(jnp.int32) for bit in range(1, count.bit_length() - 1))


def move_new(values, partner, ep_index, move_partner):
    bits = lax.axis_size("ep").bit_length() - 1

    def exchange(bit_index):
        def run(values):
            arrived = swapped(values.astype(jnp.bfloat16), "ep", bit_index)
            return jnp.where(partner == ep_index, values, arrived.astype(values.dtype))
        return run

    return lax.switch(
        chosen_case(move_partner), [exchange(bit_index) for bit_index in range(bits)], values
    )


def fused_kernel(
    bit, shifts, lag, counts_ref, partner_ref, grad_hbm, master_hbm, first_hbm, second_hbm,
    new_hbm, placed_hbm,
    grad, state, edge_out, edge_in, mid_out, mid_in, own_out, own_in, slot_out, slot_in,
    back_out, back_in, new, placed,
    load_sem, edge_send, edge_recv, mid_send, mid_recv, own_send, own_recv, rest_send, rest_recv,
    slot_send, slot_recv, back_send, back_recv, new_sem, placed_sem,
):
    parts, _, width = own_out.shape
    flat_count, capacity = grad.shape[0], state.shape[1]
    edge = flat_count - capacity
    middle = flat_count - 2 * edge
    trail = 4
    deferred = parts - (6 if bit else 0)
    low, high = jnp.bfloat16, jnp.float32
    ep_index, dp_index = lax.axis_index("ep"), lax.axis_index("dp")
    step = 1 << bit
    mate = ep_index + step * (1 - 2 * ((ep_index // step) % 2))
    to_peer, to_mate = {"dp": 1 - dp_index}, {"ep": mate}
    mesh_ids = pl.DeviceIdType.MESH

    def columns(part):
        return pl.ds(pl.multiple_of(part * width, width), width)

    def load(index):
        source = (grad_hbm, master_hbm, first_hbm, second_hbm)[index]
        target = grad if index == 0 else state.at[index - 1]
        return pltpu.make_async_copy(source, target, load_sem.at[index])

    def remote(part, rows, out, into, sent, received, target):
        return pltpu.make_async_remote_copy(
            out.at[part, :rows], into.at[part, :rows], sent.at[part], received.at[part],
            device_id=target, device_id_type=mesh_ids)

    def send_edge(part):
        return remote(part, edge, edge_out, edge_in, edge_send, edge_recv, to_peer)

    def send_mid(part, shifted):
        rows = max(middle, 3 * shifted)
        return remote(part, rows, mid_out, mid_in, mid_send, mid_recv, to_peer)

    def send_own(part, rows):
        return remote(part, rows, own_out, own_in, own_send, own_recv, to_mate)

    def send_rest(part):
        return pltpu.make_async_remote_copy(
            own_out.at[part, edge:], own_in.at[part, edge:], rest_send.at[part],
            rest_recv.at[part], device_id=to_mate, device_id_type=mesh_ids)

    def either(part, step_of):
        @pl.when(part < deferred)
        def _():
            step_of(3 * edge)

        @pl.when(part >= deferred)
        def _():
            step_of(edge)

    def send_slot(part, shifted):
        rows = 3 * max(middle - shifted, shifted)
        return remote(part, rows, slot_out, slot_in, slot_send, slot_recv, to_mate)

    def send_back(part, shifted):
        rows = edge + (max(middle - shifted, 3 * shifted) if shifted else 0)
        return remote(part, rows, back_out, back_in, back_send, back_recv, to_peer)

    def store_new(part):
        return pltpu.make_async_copy(new.at[part], new_hbm.at[:, :, columns(part)], new_sem.at[part])

    def store_placed(part):
        return pltpu.make_async_copy(
            placed.at[part], placed_hbm.at[:, columns(part)], placed_sem.at[part])

    def each(count, step_of):
        def run(group, carry):
            for index, shifted in enumerate(shifts):
                step_of(group * len(shifts) + index, shifted)
            return carry
        lax.fori_loop(0, -(-count // len(shifts)), run, 0)

    barrier = pltpu.get_barrier_semaphore()
    pl.semaphore_signal(barrier, inc=1, device_id=to_peer, device_id_type=mesh_ids)
    pl.semaphore_signal(barrier, inc=1, device_id=to_mate, device_id_type=mesh_ids)
    for index in range(4):
        load(index).start()
    pl.semaphore_wait(barrier, 2)

    source = partner_ref[ep_index]
    owns_value = counts_ref[ep_index, dp_index]
    moves_value = source
    owns_moved_value = counts_ref[source, dp_index]

    def full(value, rows):
        return jnp.broadcast_to(value, (rows, width))

    def owns(rows):
        return full(owns_value, rows) == capacity

    def owns_moved(rows):
        return full(owns_moved_value, rows) == capacity

    def moves(rows):
        return full(moves_value, rows) != ep_index

    def is_last(rows):
        return full(dp_index, rows) == 1

    def select(mask, one, other):
        return jnp.where(mask, one.astype(high), other.astype(high))

    own_edge = pl.ds(pl.multiple_of((flat_count - edge) * dp_index, edge), edge)
    peer_edge = pl.ds(pl.multiple_of((flat_count - edge) * (1 - dp_index), edge), edge)
    own_middle = pl.ds(pl.multiple_of(edge * (1 - dp_index), edge), middle)

    def update_edge(part):
        send_edge(part).wait_recv()
        held = columns(part)

        @pl.when(part == 0)
        def _():
            for index in range(1, 4):
                load(index).wait()

        edge_mean = (grad[own_edge, held] + edge_in[part].astype(high)) / 2
        late = jnp.logical_and(owns(edge), is_last(edge))
        edge_state = [
            jnp.where(late, state[index, capacity - edge:, held], state[index, :edge, held])
            for index in range(3)
        ]
        for index, result in enumerate(adam_step(edge_mean, *edge_state)):
            own_out[part, index * edge:(index + 1) * edge] = result.astype(low)
        either(part, lambda rows: send_own(part, rows).start())

    def update_middle(part, shifted):
        kept = middle - shifted
        slot_rows = max(kept, shifted)
        middle_mean = (
            grad[edge:edge + middle, columns(part)] + mid_in[part, :middle].astype(high)) / 2
        middle_state = [state[index, own_middle, columns(part)] for index in range(3)]
        for index, result in enumerate(adam_step(middle_mean, *middle_state)):
            result = result.astype(low)
            slot_out[part, index * slot_rows:index * slot_rows + kept] = result[:kept]
            if shifted:
                mid_out[part + lag, index * shifted:(index + 1) * shifted] = result[kept:]
            elif index == 0:
                mid_out[part + lag, :middle] = result

    def front(turn, shifted):
        @pl.when(turn < parts)
        def _():
            edge_out[turn] = grad[peer_edge, columns(turn)].astype(low)
            send_edge(turn).start()

        @pl.when(turn >= lag)
        def _():
            send_mid(turn - lag, shifted).wait_recv()

        @pl.when(jnp.logical_and(turn >= lag, turn < parts + lag))
        def _():
            update_middle(turn - lag, shifted)

        @pl.when(turn < lag)
        def _():
            mid_out[turn, :middle] = grad[edge:edge + middle, columns(turn)].astype(low)

        @pl.when(jnp.logical_and(turn >= lag, turn < parts))
        def _():
            mid_out[turn, :middle] = select(
                owns(middle), mid_out[turn, :middle], grad[edge:edge + middle, columns(turn)]).astype(low)

        @pl.when(turn < parts + lag)
        def _():
            send_mid(turn, shifted).start()

        @pl.when(jnp.logical_and(turn >= 1, turn < parts + 1))
        def _():
            update_edge(turn - 1)

        @pl.when(turn >= 2 * lag)
        def _():
            part = turn - 2 * lag
            slot_rows = max(middle - shifted, shifted)
            pieces = [(index * slot_rows, index * shifted, shifted) for index in range(3)]
            for at, come, rows in pieces if shifted else [(0, 0, middle)]:
                slot_out[part, at:at + rows] = select(
                    owns(rows), slot_out[part, at:at + rows],
                    mid_in[turn - lag, come:come + rows]).astype(low)
            send_slot(part, shifted).start()

    load(0).wait()
    each(parts + 2 * lag, front)

    def later(step_of):
        def run(part, carry):
            step_of(part)
            return carry
        lax.fori_loop(deferred, parts, run, 0)

    later(lambda part: send_rest(part).start())

    def arrive(part, shifted):
        slot_rows = max(middle - shifted, shifted)
        def take(rows):
            send_own(part, rows).wait_recv()
            own_in[part, :rows] = select(
                moves(rows), own_in[part, :rows], own_out[part, :rows]).astype(low)

        either(part, take)
        back_out[part, :edge] = own_in[part, :edge]
        send_slot(part, shifted).wait_recv()
        rows = 3 * slot_rows
        slot_in[part, :rows] = select(
            moves(rows), slot_in[part, :rows], slot_out[part, :rows]).astype(low)
        if shifted:
            for index in range(3):
                at = index * shifted
                back_out[part, edge + at:edge + at + shifted] = select(
                    owns_moved(shifted), slot_in[part, at:at + shifted],
                    slot_in[part, index * slot_rows:index * slot_rows + shifted]).astype(low)
        send_back(part, shifted).start()

    def place(part, shifted):
        either(part, functools.partial(place_with, part, shifted))

    def place_with(part, shifted, ready):
        kept = middle - shifted
        slot_rows = max(kept, shifted)
        send_back(part, shifted).wait_recv()
        keeps, last = owns_moved(edge), is_last(edge)
        zero = jnp.zeros((edge, width), high)
        for index in range(3):
            held = slot_in[part, index * slot_rows:index * slot_rows + kept].astype(high)
            if shifted:
                rest = back_in[part, edge + index * shifted:edge + (index + 1) * shifted]
                moved = jnp.concatenate([held, rest.astype(high)], axis=0)
            else:
                moved = held
            ends = zero
            if index * edge < ready:
                ends = own_in[part, index * edge:(index + 1) * edge].astype(high)
            low_half, high_half = moved[:edge], moved[edge:]
            new[part, index, :edge] = jnp.where(
                jnp.logical_and(keeps, last), low_half, ends).astype(low)
            new[part, index, edge:2 * edge] = jnp.where(
                keeps, jnp.where(last, high_half, low_half), zero).astype(low)
            new[part, index, 2 * edge:] = jnp.where(
                keeps, jnp.where(last, ends, high_half), zero).astype(low)
            if index == 0:
                if shifted:
                    other = jnp.concatenate([
                        back_in[part, edge:edge + kept].astype(high),
                        slot_in[part, :shifted].astype(high)], axis=0)
                    moved = jnp.where(owns_moved(middle), moved, other)
                placed[part, edge:edge + middle] = moved.astype(low)
                peer_ends = back_in[part, :edge].astype(high)
                placed[part, :edge] = jnp.where(last, peer_ends, ends).astype(low)
                placed[part, edge + middle:] = jnp.where(last, ends, peer_ends).astype(low)
        if ready > edge:
            store_new(part).start()
        store_placed(part).start()

    def place_rest(part):
        send_rest(part).wait_recv()
        late = jnp.logical_and(owns_moved(edge), is_last(edge))
        for index in (1, 2):
            rows = slice(index * edge, (index + 1) * edge)
            ends = select(moves(edge), own_in[part, rows], own_out[part, rows])
            new[part, index, :edge] = select(late, new[part, index, :edge], ends).astype(low)
            new[part, index, 2 * edge:] = select(
                late, ends, new[part, index, 2 * edge:]).astype(low)
        store_new(part).start()

    def finish(part, shifted):
        send_edge(part).wait_send()
        send_mid(part, shifted).wait_send()
        either(part, lambda rows: send_own(part, rows).wait_send())
        send_slot(part, shifted).wait_send()
        send_back(part, shifted).wait_send()
        store_placed(part).wait()

        @pl.when(part < deferred)
        def _():
            store_new(part).wait()

    def back(turn, shifted):
        @pl.when(turn < parts)
        def _():
            arrive(turn, shifted)

        @pl.when(jnp.logical_and(turn > 0, turn <= parts))
        def _():
            place(turn - 1, shifts[shifts.index(shifted) - 1])

        @pl.when(turn >= trail)
        def _():
            finish(turn - trail, shifted)

    each(parts + trail, back)
    each(lag, lambda part, shifted: send_mid(parts + part, shifted).wait_send())
    later(place_rest)

    def finish_rest(part):
        send_rest(part).wait_send()
        store_new(part).wait()

    later(finish_rest)


def fused(bit, shifts, counts, partner, gradients, master, first, second):
    flat_count, model = gradients.shape
    capacity = master.shape[0]
    edge = flat_count - capacity
    middle = flat_count - 2 * edge
    width, lag = 512, 2
    parts = model // width
    mid_rows = max(max(middle, 3 * shifted) for shifted in shifts)
    slot_rows = max(3 * max(middle - shifted, shifted) for shifted in shifts)
    back_rows = edge + max(
        max(middle - shifted, 3 * shifted) if shifted else 0 for shifted in shifts)
    low, high = jnp.bfloat16, jnp.float32
    sems, more_sems = (pltpu.SemaphoreType.DMA((count,)) for count in (parts, parts + lag))
    smem = pl.BlockSpec(memory_space=pltpu.SMEM)
    anywhere = pl.BlockSpec(memory_space=pl.ANY)

    def pair(count, rows):
        return [pltpu.VMEM((count, rows, width), low)] * 2

    return pl.pallas_call(
        functools.partial(fused_kernel, bit, shifts, lag),
        out_shape=(
            jax.ShapeDtypeStruct((3, capacity, model), low),
            jax.ShapeDtypeStruct((flat_count, model), low),
        ),
        in_specs=[smem, smem] + [anywhere] * 4,
        out_specs=(anywhere, anywhere),
        scratch_shapes=[
            pltpu.VMEM((flat_count, model), high),
            pltpu.VMEM((3, capacity, model), high),
        ] + pair(parts, edge) + pair(parts + lag, mid_rows) + pair(parts, 3 * edge)
        + pair(parts, slot_rows) + pair(parts, back_rows) + [
            pltpu.VMEM((parts, 3, capacity, width), low),
            pltpu.VMEM((parts, flat_count, width), low),
            pltpu.SemaphoreType.DMA((4,)),
        ] + [sems] * 2 + [more_sems] * 2 + [sems] * 10,
        compiler_params=pltpu.CompilerParams(
            collective_id=bit, has_side_effects=True, vmem_limit_bytes=38 * 1024 * 1024),
        name=f"fused_bit_{bit}",
    )(counts, partner, gradients, master, first, second)


def body_pairs(gradients, master_rows, first_moment, second_moment, shard_rows, move_partner):
    bits = lax.axis_size("ep").bit_length() - 1
    moved, placed = lax.switch(
        chosen_case(move_partner),
        [functools.partial(fused, bit, shifts_of_bit[bit]) for bit in range(bits)],
        shard_rows, move_partner, gradients[0], master_rows[0], first_moment[0], second_moment[0],
    )
    wide = moved.astype(jnp.float32)
    return (wide[0][None], wide[1][None], wide[2][None], placed)


def body(gradients, master_rows, first_moment, second_moment, shard_rows, move_partner):
    groups = lax.axis_size("dp")
    capacity = master_rows.shape[1]
    flat_count = gradients.shape[1]
    dp_index = lax.axis_index("dp")
    ep_index = lax.axis_index("ep")
    partner = move_partner[ep_index]
    counts = shard_rows[ep_index]
    moved_counts = shard_rows[partner]
    starts = jnp.cumsum(counts) - counts
    moved_starts = jnp.cumsum(moved_counts) - moved_counts
    own_slots = jnp.arange(capacity, dtype=jnp.int32)
    live = (own_slots < counts[dp_index])[:, None]
    state = jnp.stack([master_rows[0], first_moment[0], second_moment[0]])
    slots = jnp.arange(groups * capacity, dtype=jnp.int32)
    owners = slots // capacity
    within = slots % capacity
    live_all = (within < counts[owners])[:, None]
    source = jnp.minimum(starts[owners] + within, flat_count - 1)
    packed = jnp.where(live_all, jnp.take(gradients[0], source, axis=0), 0.0)
    summed = lax.psum_scatter(
        packed.astype(jnp.bfloat16), "dp", scatter_dimension=0, tiled=True
    ).astype(jnp.float32)
    grad_own = summed / groups
    stepped = jnp.where(live, jnp.stack(adam_step(grad_own, state[0], state[1], state[2])), 0.0)
    moved = move_new(stepped, partner, ep_index, move_partner)
    updated, first_new, second_new = (moved[0], moved[1], moved[2])
    whole = lax.all_gather(updated.astype(jnp.bfloat16), "dp", axis=0, tiled=True)
    flat_rows = jnp.arange(flat_count, dtype=jnp.int32)
    owner_flat = jnp.sum((flat_rows[:, None] >= moved_starts[None, 1:]).astype(jnp.int32), axis=1)
    position = owner_flat * capacity + flat_rows - moved_starts[owner_flat]
    placed = jnp.take(whole, position, axis=0)
    return (updated[None], first_new[None], second_new[None], placed)


def solution(mesh):
    placed = (
        P("dp", "ep", None),
        P("ep", "dp", None),
        P("ep", "dp", None),
        P("ep", "dp", None),
        P(),
        P(),
    )
    return jax.shard_map(
        body_pairs if mesh.shape["dp"] == 2 else body,
        mesh=mesh,
        in_specs=placed,
        out_specs=(P("ep", "dp", None), P("ep", "dp", None), P("ep", "dp", None), P("ep", None)),
        check_vma=False,
    )
```

```python
import functools

import jax
import jax.numpy as jnp
from jax import lax
from jax.experimental import pallas as pl
from jax.experimental.pallas import tpu as pltpu
from jax.sharding import PartitionSpec as P

beta_one = 0.9
beta_two = 0.95
learn_rate = 0.02
weight_decay = 0.1
epsilon = 1e-08
shifts_of_bit = ((0,), (16, 32), (16, 32), (32,))
correct_one = 1.0 - 0.9**10
correct_two = 1.0 - 0.95**10


def swapped(array, axis, apart):
    return lax.ppermute(array, axis, [(i, i ^ 1 << apart) for i in range(lax.axis_size(axis))])


def adam_step(grad_rows, weights, first, second):
    first_new = beta_one * first + (1.0 - beta_one) * grad_rows
    second_new = beta_two * second + (1.0 - beta_two) * grad_rows * grad_rows
    ratio = first_new / correct_one / (jnp.sqrt(second_new / correct_two) + epsilon)
    updated = weights - learn_rate * (ratio + weight_decay * weights)
    return updated, first_new, second_new


def chosen_case(move_partner):
    count = move_partner.shape[0]
    flips = jnp.bitwise_xor(move_partner, jnp.arange(count, dtype=jnp.int32))
    digit = jnp.max(flips)
    return sum((digit >= 1 << bit).astype(jnp.int32) for bit in range(1, count.bit_length() - 1))


def move_new(values, partner, ep_index, move_partner):
    bits = lax.axis_size("ep").bit_length() - 1

    def exchange(bit_index):
        def run(values):
            arrived = swapped(values.astype(jnp.bfloat16), "ep", bit_index)
            return jnp.where(partner == ep_index, values, arrived.astype(values.dtype))
        return run

    return lax.switch(
        chosen_case(move_partner), [exchange(bit_index) for bit_index in range(bits)], values
    )


def fused_kernel(
    bit, shifts, lag, counts_ref, partner_ref, grad_hbm, master_hbm, first_hbm, second_hbm,
    new_hbm, placed_hbm,
    grad, state, edge_out, edge_in, mid_out, mid_in, own_out, own_in, slot_out, slot_in,
    back_out, back_in, new, placed,
    load_sem, edge_send, edge_recv, mid_send, mid_recv, own_send, own_recv, rest_send, rest_recv,
    slot_send, slot_recv, back_send, back_recv, new_sem, placed_sem,
):
    parts, _, width = own_out.shape
    flat_count, capacity = grad.shape[0], state.shape[1]
    edge = flat_count - capacity
    middle = flat_count - 2 * edge
    trail = 4
    deferred = parts - (6 if bit else 0)
    low, high = jnp.bfloat16, jnp.float32
    ep_index, dp_index = lax.axis_index("ep"), lax.axis_index("dp")
    step = 1 << bit
    mate = ep_index + step * (1 - 2 * ((ep_index // step) % 2))
    to_peer, to_mate = {"dp": 1 - dp_index}, {"ep": mate}
    mesh_ids = pl.DeviceIdType.MESH

    def columns(part):
        return pl.ds(pl.multiple_of(part * width, width), width)

    def load(index):
        source = (grad_hbm, master_hbm, first_hbm, second_hbm)[index]
        target = grad if index == 0 else state.at[index - 1]
        return pltpu.make_async_copy(source, target, load_sem.at[index])

    def remote(part, rows, out, into, sent, received, target):
        return pltpu.make_async_remote_copy(
            out.at[part, :rows], into.at[part, :rows], sent.at[part], received.at[part],
            device_id=target, device_id_type=mesh_ids)

    def send_edge(part):
        return remote(part, edge, edge_out, edge_in, edge_send, edge_recv, to_peer)

    def send_mid(part, shifted):
        rows = max(middle, 3 * shifted)
        return remote(part, rows, mid_out, mid_in, mid_send, mid_recv, to_peer)

    def send_own(part, rows):
        return remote(part, rows, own_out, own_in, own_send, own_recv, to_mate)

    def send_rest(part):
        return pltpu.make_async_remote_copy(
            own_out.at[part, edge:], own_in.at[part, edge:], rest_send.at[part],
            rest_recv.at[part], device_id=to_mate, device_id_type=mesh_ids)

    def either(part, step_of):
        @pl.when(part < deferred)
        def _():
            step_of(3 * edge)

        @pl.when(part >= deferred)
        def _():
            step_of(edge)

    def send_slot(part, shifted):
        rows = 3 * max(middle - shifted, shifted)
        return remote(part, rows, slot_out, slot_in, slot_send, slot_recv, to_mate)

    def send_back(part, shifted):
        rows = edge + (max(middle - shifted, 3 * shifted) if shifted else 0)
        return remote(part, rows, back_out, back_in, back_send, back_recv, to_peer)

    def store_new(part):
        return pltpu.make_async_copy(new.at[part], new_hbm.at[:, :, columns(part)], new_sem.at[part])

    def store_placed(part):
        return pltpu.make_async_copy(
            placed.at[part], placed_hbm.at[:, columns(part)], placed_sem.at[part])

    def each(count, step_of):
        def run(group, carry):
            for index, shifted in enumerate(shifts):
                step_of(group * len(shifts) + index, shifted)
            return carry
        lax.fori_loop(0, -(-count // len(shifts)), run, 0)

    barrier = pltpu.get_barrier_semaphore()
    pl.semaphore_signal(barrier, inc=1, device_id=to_peer, device_id_type=mesh_ids)
    pl.semaphore_signal(barrier, inc=1, device_id=to_mate, device_id_type=mesh_ids)
    for index in range(4):
        load(index).start()
    pl.semaphore_wait(barrier, 2)

    source = partner_ref[ep_index]
    owns_value = counts_ref[ep_index, dp_index]
    moves_value = source
    owns_moved_value = counts_ref[source, dp_index]

    def full(value, rows):
        return jnp.broadcast_to(value, (rows, width))

    def owns(rows):
        return full(owns_value, rows) == capacity

    def owns_moved(rows):
        return full(owns_moved_value, rows) == capacity

    def moves(rows):
        return full(moves_value, rows) != ep_index

    def is_last(rows):
        return full(dp_index, rows) == 1

    def select(mask, one, other):
        return jnp.where(mask, one.astype(high), other.astype(high))

    own_edge = pl.ds(pl.multiple_of((flat_count - edge) * dp_index, edge), edge)
    peer_edge = pl.ds(pl.multiple_of((flat_count - edge) * (1 - dp_index), edge), edge)
    own_middle = pl.ds(pl.multiple_of(edge * (1 - dp_index), edge), middle)

    def update_edge(part):
        send_edge(part).wait_recv()
        held = columns(part)

        @pl.when(part == 0)
        def _():
            for index in range(1, 4):
                load(index).wait()

        edge_mean = (grad[own_edge, held] + edge_in[part].astype(high)) / 2
        late = jnp.logical_and(owns(edge), is_last(edge))
        edge_state = [
            jnp.where(late, state[index, capacity - edge:, held], state[index, :edge, held])
            for index in range(3)
        ]
        for index, result in enumerate(adam_step(edge_mean, *edge_state)):
            own_out[part, index * edge:(index + 1) * edge] = result.astype(low)
        either(part, lambda rows: send_own(part, rows).start())

    def update_middle(part, shifted):
        kept = middle - shifted
        slot_rows = max(kept, shifted)
        middle_mean = (
            grad[edge:edge + middle, columns(part)] + mid_in[part, :middle].astype(high)) / 2
        middle_state = [state[index, own_middle, columns(part)] for index in range(3)]
        for index, result in enumerate(adam_step(middle_mean, *middle_state)):
            result = result.astype(low)
            slot_out[part, index * slot_rows:index * slot_rows + kept] = result[:kept]
            if shifted:
                mid_out[part + lag, index * shifted:(index + 1) * shifted] = result[kept:]
            elif index == 0:
                mid_out[part + lag, :middle] = result

    def front(turn, shifted):
        @pl.when(turn < parts)
        def _():
            edge_out[turn] = grad[peer_edge, columns(turn)].astype(low)
            send_edge(turn).start()

        @pl.when(turn >= lag)
        def _():
            send_mid(turn - lag, shifted).wait_recv()

        @pl.when(jnp.logical_and(turn >= lag, turn < parts + lag))
        def _():
            update_middle(turn - lag, shifted)

        @pl.when(turn < lag)
        def _():
            mid_out[turn, :middle] = grad[edge:edge + middle, columns(turn)].astype(low)

        @pl.when(jnp.logical_and(turn >= lag, turn < parts))
        def _():
            mid_out[turn, :middle] = select(
                owns(middle), mid_out[turn, :middle], grad[edge:edge + middle, columns(turn)]).astype(low)

        @pl.when(turn < parts + lag)
        def _():
            send_mid(turn, shifted).start()

        @pl.when(jnp.logical_and(turn >= 1, turn < parts + 1))
        def _():
            update_edge(turn - 1)

        @pl.when(turn >= 2 * lag)
        def _():
            part = turn - 2 * lag
            slot_rows = max(middle - shifted, shifted)
            pieces = [(index * slot_rows, index * shifted, shifted) for index in range(3)]
            for at, come, rows in pieces if shifted else [(0, 0, middle)]:
                slot_out[part, at:at + rows] = select(
                    owns(rows), slot_out[part, at:at + rows],
                    mid_in[turn - lag, come:come + rows]).astype(low)
            send_slot(part, shifted).start()

    load(0).wait()
    each(parts + 2 * lag, front)

    def later(step_of):
        def run(part, carry):
            step_of(part)
            return carry
        lax.fori_loop(deferred, parts, run, 0)

    later(lambda part: send_rest(part).start())

    def arrive(part, shifted):
        slot_rows = max(middle - shifted, shifted)
        def take(rows):
            send_own(part, rows).wait_recv()
            own_in[part, :rows] = select(
                moves(rows), own_in[part, :rows], own_out[part, :rows]).astype(low)

        either(part, take)
        back_out[part, :edge] = own_in[part, :edge]
        send_slot(part, shifted).wait_recv()
        rows = 3 * slot_rows
        slot_in[part, :rows] = select(
            moves(rows), slot_in[part, :rows], slot_out[part, :rows]).astype(low)
        if shifted:
            for index in range(3):
                at = index * shifted
                back_out[part, edge + at:edge + at + shifted] = select(
                    owns_moved(shifted), slot_in[part, at:at + shifted],
                    slot_in[part, index * slot_rows:index * slot_rows + shifted]).astype(low)
        send_back(part, shifted).start()

    def place(part, shifted):
        either(part, functools.partial(place_with, part, shifted))

    def place_with(part, shifted, ready):
        kept = middle - shifted
        slot_rows = max(kept, shifted)
        send_back(part, shifted).wait_recv()
        keeps, last = owns_moved(edge), is_last(edge)
        zero = jnp.zeros((edge, width), high)
        for index in range(3):
            held = slot_in[part, index * slot_rows:index * slot_rows + kept].astype(high)
            if shifted:
                rest = back_in[part, edge + index * shifted:edge + (index + 1) * shifted]
                moved = jnp.concatenate([held, rest.astype(high)], axis=0)
            else:
                moved = held
            ends = zero
            if index * edge < ready:
                ends = own_in[part, index * edge:(index + 1) * edge].astype(high)
            low_half, high_half = moved[:edge], moved[edge:]
            new[part, index, :edge] = jnp.where(
                jnp.logical_and(keeps, last), low_half, ends).astype(low)
            new[part, index, edge:2 * edge] = jnp.where(
                keeps, jnp.where(last, high_half, low_half), zero).astype(low)
            new[part, index, 2 * edge:] = jnp.where(
                keeps, jnp.where(last, ends, high_half), zero).astype(low)
            if index == 0:
                if shifted:
                    other = jnp.concatenate([
                        back_in[part, edge:edge + kept].astype(high),
                        slot_in[part, :shifted].astype(high)], axis=0)
                    moved = jnp.where(owns_moved(middle), moved, other)
                placed[part, edge:edge + middle] = moved.astype(low)
                peer_ends = back_in[part, :edge].astype(high)
                placed[part, :edge] = jnp.where(last, peer_ends, ends).astype(low)
                placed[part, edge + middle:] = jnp.where(last, ends, peer_ends).astype(low)
        if ready > edge:
            store_new(part).start()
        store_placed(part).start()

    def place_rest(part):
        send_rest(part).wait_recv()
        late = jnp.logical_and(owns_moved(edge), is_last(edge))
        for index in (1, 2):
            rows = slice(index * edge, (index + 1) * edge)
            ends = select(moves(edge), own_in[part, rows], own_out[part, rows])
            new[part, index, :edge] = select(late, new[part, index, :edge], ends).astype(low)
            new[part, index, 2 * edge:] = select(
                late, ends, new[part, index, 2 * edge:]).astype(low)
        store_new(part).start()

    def finish(part, shifted):
        send_edge(part).wait_send()
        send_mid(part, shifted).wait_send()
        either(part, lambda rows: send_own(part, rows).wait_send())
        send_slot(part, shifted).wait_send()
        send_back(part, shifted).wait_send()
        store_placed(part).wait()

        @pl.when(part < deferred)
        def _():
            store_new(part).wait()

    def back(turn, shifted):
        @pl.when(turn < parts)
        def _():
            arrive(turn, shifted)

        @pl.when(jnp.logical_and(turn > 0, turn <= parts))
        def _():
            place(turn - 1, shifts[shifts.index(shifted) - 1])

        @pl.when(turn >= trail)
        def _():
            finish(turn - trail, shifted)

    each(parts + trail, back)
    each(lag, lambda part, shifted: send_mid(parts + part, shifted).wait_send())
    later(place_rest)

    def finish_rest(part):
        send_rest(part).wait_send()
        store_new(part).wait()

    later(finish_rest)


def fused(bit, shifts, counts, partner, gradients, master, first, second):
    flat_count, model = gradients.shape
    capacity = master.shape[0]
    edge = flat_count - capacity
    middle = flat_count - 2 * edge
    width, lag = 512, 4
    parts = model // width
    mid_rows = max(max(middle, 3 * shifted) for shifted in shifts)
    slot_rows = max(3 * max(middle - shifted, shifted) for shifted in shifts)
    back_rows = edge + max(
        max(middle - shifted, 3 * shifted) if shifted else 0 for shifted in shifts)
    low, high = jnp.bfloat16, jnp.float32
    sems, more_sems = (pltpu.SemaphoreType.DMA((count,)) for count in (parts, parts + lag))
    smem = pl.BlockSpec(memory_space=pltpu.SMEM)
    anywhere = pl.BlockSpec(memory_space=pl.ANY)

    def pair(count, rows):
        return [pltpu.VMEM((count, rows, width), low)] * 2

    return pl.pallas_call(
        functools.partial(fused_kernel, bit, shifts, lag),
        out_shape=(
            jax.ShapeDtypeStruct((3, capacity, model), low),
            jax.ShapeDtypeStruct((flat_count, model), low),
        ),
        in_specs=[smem, smem] + [anywhere] * 4,
        out_specs=(anywhere, anywhere),
        scratch_shapes=[
            pltpu.VMEM((flat_count, model), high),
            pltpu.VMEM((3, capacity, model), high),
        ] + pair(parts, edge) + pair(parts + lag, mid_rows) + pair(parts, 3 * edge)
        + pair(parts, slot_rows) + pair(parts, back_rows) + [
            pltpu.VMEM((parts, 3, capacity, width), low),
            pltpu.VMEM((parts, flat_count, width), low),
            pltpu.SemaphoreType.DMA((4,)),
        ] + [sems] * 2 + [more_sems] * 2 + [sems] * 10,
        compiler_params=pltpu.CompilerParams(
            collective_id=bit, has_side_effects=True, vmem_limit_bytes=38 * 1024 * 1024),
        name=f"fused_bit_{bit}",
    )(counts, partner, gradients, master, first, second)


def body_pairs(gradients, master_rows, first_moment, second_moment, shard_rows, move_partner):
    bits = lax.axis_size("ep").bit_length() - 1
    moved, placed = lax.switch(
        chosen_case(move_partner),
        [functools.partial(fused, bit, shifts_of_bit[bit]) for bit in range(bits)],
        shard_rows, move_partner, gradients[0], master_rows[0], first_moment[0], second_moment[0],
    )
    wide = moved.astype(jnp.float32)
    return (wide[0][None], wide[1][None], wide[2][None], placed)


def body(gradients, master_rows, first_moment, second_moment, shard_rows, move_partner):
    groups = lax.axis_size("dp")
    capacity = master_rows.shape[1]
    flat_count = gradients.shape[1]
    dp_index = lax.axis_index("dp")
    ep_index = lax.axis_index("ep")
    partner = move_partner[ep_index]
    counts = shard_rows[ep_index]
    moved_counts = shard_rows[partner]
    starts = jnp.cumsum(counts) - counts
    moved_starts = jnp.cumsum(moved_counts) - moved_counts
    own_slots = jnp.arange(capacity, dtype=jnp.int32)
    live = (own_slots < counts[dp_index])[:, None]
    state = jnp.stack([master_rows[0], first_moment[0], second_moment[0]])
    slots = jnp.arange(groups * capacity, dtype=jnp.int32)
    owners = slots // capacity
    within = slots % capacity
    live_all = (within < counts[owners])[:, None]
    source = jnp.minimum(starts[owners] + within, flat_count - 1)
    packed = jnp.where(live_all, jnp.take(gradients[0], source, axis=0), 0.0)
    summed = lax.psum_scatter(
        packed.astype(jnp.bfloat16), "dp", scatter_dimension=0, tiled=True
    ).astype(jnp.float32)
    grad_own = summed / groups
    stepped = jnp.where(live, jnp.stack(adam_step(grad_own, state[0], state[1], state[2])), 0.0)
    moved = move_new(stepped, partner, ep_index, move_partner)
    updated, first_new, second_new = (moved[0], moved[1], moved[2])
    whole = lax.all_gather(updated.astype(jnp.bfloat16), "dp", axis=0, tiled=True)
    flat_rows = jnp.arange(flat_count, dtype=jnp.int32)
    owner_flat = jnp.sum((flat_rows[:, None] >= moved_starts[None, 1:]).astype(jnp.int32), axis=1)
    position = owner_flat * capacity + flat_rows - moved_starts[owner_flat]
    placed = jnp.take(whole, position, axis=0)
    return (updated[None], first_new[None], second_new[None], placed)


def solution(mesh):
    placed = (
        P("dp", "ep", None),
        P("ep", "dp", None),
        P("ep", "dp", None),
        P("ep", "dp", None),
        P(),
        P(),
    )
    return jax.shard_map(
        body_pairs if mesh.shape["dp"] == 2 else body,
        mesh=mesh,
        in_specs=placed,
        out_specs=(P("ep", "dp", None), P("ep", "dp", None), P("ep", "dp", None), P("ep", None)),
        check_vma=False,
    )
```
